128 devices in a mesh: ctx: 32 (over z, y, core), fsdp: 4 (over x).
Axes of the slice: x: 4, y: 4, z: 4, core: 2. Of those that a mesh axis runs over, the one named last changes fastest.
Arguments:
- tokens: bfloat16 [4, 4096, 576], P('fsdp', 'ctx'), may hold values from -6 to 6
- pairing: int32 [64], replicated, may hold values from 0 to 63, as said below
- cotangent: float32 [4, 4096, 576], P('fsdp', 'ctx'), may hold values from -6 to 6
- w_query: bfloat16 [2, 576, 576], P(None, 'fsdp'), may hold values from -0.25 to 0.25
- key_projection_weight: bfloat16 [2, 576, 192], P(None, 'fsdp'), may hold values from -0.25 to 0.25
- value_projection_weight: bfloat16 [2, 576, 192], P(None, 'fsdp'), may hold values from -0.25 to 0.25
- w_out: bfloat16 [2, 576, 576], P(None, 'fsdp'), may hold values from -6 to 6
- w_gate: bfloat16 [2, 576, 1536], P(None, None, 'fsdp'), may hold values from -0.25 to 0.25
- w_up: bfloat16 [2, 576, 1536], P(None, None, 'fsdp'), may hold values from -0.25 to 0.25
- w_down: bfloat16 [2, 1536, 576], P(None, 'fsdp'), may hold values from -0.15625 to 0.15625
- attn_gain: bfloat16 [2, 576], P(None, 'fsdp'), may hold values from 0.099609375 to 1.8984375
- ffn_gain: bfloat16 [2, 576], P(None, 'fsdp'), may hold values from 0.099609375 to 1.8984375
Outputs:
- out: float32 [4, 4096, 576], P('fsdp', 'ctx')
- d_tokens: float32 [4, 4096, 576], P('fsdp', 'ctx')
- d_w_query: float32 [2, 576, 576], P(None, 'fsdp')
- d_w_key: float32 [2, 576, 192], P(None, 'fsdp')
- d_w_value: float32 [2, 576, 192], P(None, 'fsdp')
- d_w_out: float32 [2, 576, 576], P(None, 'fsdp')
- d_w_gate: float32 [2, 576, 1536], P(None, None, 'fsdp')
- d_w_up: float32 [2, 576, 1536], P(None, None, 'fsdp')
- d_w_down: float32 [2, 1536, 576], P(None, 'fsdp')
- d_attn_gain: float32 [2, 576], P(None, 'fsdp')
- d_ffn_gain: float32 [2, 576], P(None, 'fsdp')
The draws below stay inside these ranges and needn't reach their ends.
Inputs may be any that keep to these rules, and one draw needn't show every extreme that they name: `pairing`: every value appears once. Entries 2 c and 2 c + 1 are the position blocks of storage blocks 2 c and 2 c + 1; they add up to 63.
All inputs are finite; a program needn't handle non-finite values.
Results may differ from the reference program's by a relative error of at most 0.03.
Values may be sent and summed in bfloat16 or wider, within the bound.
No kernel may reach another device: no remote copies, remote signals or barrier semaphores. Data moves between devices by JAX's collectives and lax.ppermute only.
A program may use at most 128 MiB of HBM per device.

```python
import jax
import jax.numpy as jnp
from jax import lax

MODEL_DIM = 576
QUERY_HEADS = 9
KEY_VALUE_HEADS = 3
HEAD_SIZE = 64
FF = 1536
BLK = 64
DECODER_LAYERS = 2
BLOCKS = 64
SEQLEN = 4096
SEQS = 4


def draw_pairing(key, part):
    half_count = BLOCKS // 2
    order = jax.random.permutation(key, half_count).astype(jnp.int32)
    flips = jax.random.randint(jax.random.fold_in(key, 7), (half_count,), 0, 2)
    first_block = jnp.where(flips == 1, BLOCKS - 1 - order, order)
    return jnp.stack([first_block, BLOCKS - 1 - first_block], axis=1).reshape(BLOCKS).astype(jnp.int32)


def block_levels(rng, extent, split, low, top_value):
    factor_of = 1.0
    for position, parts in split:
        heights = jax.random.uniform(jax.random.fold_in(jax.random.fold_in(rng, 6), position), (parts,), jnp.float32, low / len(split), top_value / len(split))
        factor_of = factor_of * jnp.repeat(jnp.exp(heights), extent[position] // parts).reshape((-1,) + (1,) * (len(extent) - 1 - position))
    return factor_of


def centred(key, shape, scale, reach, pieces=(), kind=jnp.bfloat16):
    factor_of = block_levels(key, shape, pieces, -0.22, 0.18) if pieces else 1.0
    values = jax.random.normal(key, shape, jnp.float32) * scale * factor_of
    return jnp.minimum(jnp.maximum(values, -reach), reach).astype(kind)


def setup_inputs(seed: int = 0) -> dict:
    arg_keys = jax.random.split(jax.random.key(seed), 13)
    tokens = centred(arg_keys[0], (SEQS, SEQLEN, MODEL_DIM), 1.0, 6.0, ((0, 4), (1, 32)))
    pairing = draw_pairing(jax.random.fold_in(arg_keys[12], 71), 0)
    cotangent = centred(arg_keys[2], (SEQS, SEQLEN, MODEL_DIM), 1.0, 6.0, ((0, 4), (1, 32)), jnp.float32)
    w_query = centred(arg_keys[3], (DECODER_LAYERS, MODEL_DIM, QUERY_HEADS * HEAD_SIZE), MODEL_DIM ** -0.5, 0.25, ((1, 4),))
    key_projection_weight = centred(arg_keys[4], (DECODER_LAYERS, MODEL_DIM, KEY_VALUE_HEADS * HEAD_SIZE), MODEL_DIM ** -0.5, 0.25, ((1, 4),))
    value_projection_weight = centred(arg_keys[5], (DECODER_LAYERS, MODEL_DIM, KEY_VALUE_HEADS * HEAD_SIZE), MODEL_DIM ** -0.5, 0.25, ((1, 4),))
    w_out = centred(arg_keys[6], (DECODER_LAYERS, QUERY_HEADS * HEAD_SIZE, MODEL_DIM), (max(1, 3072 // SEQLEN)) ** -0.5, 6.0, ((1, 4),))
    w_gate = centred(arg_keys[7], (DECODER_LAYERS, MODEL_DIM, FF), MODEL_DIM ** -0.5, 0.25, ((2, 4),))
    w_up = centred(arg_keys[8], (DECODER_LAYERS, MODEL_DIM, FF), MODEL_DIM ** -0.5, 0.25, ((2, 4),))
    w_down = centred(arg_keys[9], (DECODER_LAYERS, FF, MODEL_DIM), FF ** -0.5, 0.15625, ((1, 4),))
    attn_gain = jnp.clip(1.0 + 0.18 * jax.random.normal(arg_keys[10], (DECODER_LAYERS, MODEL_DIM), jnp.float32), 0.099609375, 1.8984375).astype(jnp.bfloat16)
    ffn_gain = jnp.clip(1.0 + 0.18 * jax.random.normal(arg_keys[11], (DECODER_LAYERS, MODEL_DIM), jnp.float32), 0.099609375, 1.8984375).astype(jnp.bfloat16)
    return dict(tokens=tokens, pairing=pairing, cotangent=cotangent, w_query=w_query, key_projection_weight=key_projection_weight, value_projection_weight=value_projection_weight, w_out=w_out, w_gate=w_gate, w_up=w_up, w_down=w_down, attn_gain=attn_gain, ffn_gain=ffn_gain)


epsilon = 1e-05
rope_base = 100000.0
negative = -1e+30

@jax.custom_vjp
def lower_precision(v):
    return lax.optimization_barrier(v.astype(jnp.bfloat16)).astype(jnp.float32)

@jax.custom_vjp
def lower_precision_backward(v):
    return v

def low_keep(v):
    return (lower_precision(v), None)

def low_pass(kept, grad):
    return (grad,)

def back_keep(v):
    return (v, None)

def back_low(kept, grad):
    return (lower_precision(grad),)
lower_precision.defvjp(low_keep, low_pass)
lower_precision_backward.defvjp(back_keep, back_low)

def angles(positions):
    half_dim = HEAD_SIZE // 2
    frequency = rope_base ** (-(jnp.arange(half_dim, dtype=jnp.float32) * 2.0 / HEAD_SIZE))
    return positions.astype(jnp.float32)[:, None] * frequency[None, :]

def rotary_apply(values, angle_table):
    half_dim = values.shape[-1] // 2
    cos_part = jnp.cos(angle_table)[:, None, :]
    sin_part = jnp.sin(angle_table)[:, None, :]
    first_half = values[..., :half_dim]
    second_half = values[..., half_dim:]
    return jnp.concatenate([first_half * cos_part - second_half * sin_part, second_half * cos_part + first_half * sin_part], axis=-1)

def product_float32(incoming_rows, weight_matrix):
    return jnp.einsum('aqu,uo->aqo', incoming_rows, weight_matrix, precision=lax.Precision.HIGHEST)

def normalize(stream, gain):
    return stream * lax.rsqrt(lax.optimization_barrier(jnp.mean(stream * stream, axis=-1, keepdims=True)) + epsilon) * gain

def attend(query_input, keys, values, positions):
    sequence_length = query_input.shape[0]
    rows_per_block = min(512, sequence_length)
    query_block_list = query_input.reshape(sequence_length // rows_per_block, rows_per_block, KEY_VALUE_HEADS, QUERY_HEADS // KEY_VALUE_HEADS, HEAD_SIZE)
    position_blocks = positions.reshape(sequence_length // rows_per_block, rows_per_block)

    def block_attention(pair):
        query_block, query_pos = pair
        raw = jnp.einsum('qgrd,kgd->grqk', query_block, keys, precision=lax.Precision.HIGHEST) * HEAD_SIZE ** (-0.5)
        raw = lower_precision_backward(raw)
        masked = jnp.where(positions[None, None, None, :] <= query_pos[None, None, :, None], raw, negative)
        biggest = lax.optimization_barrier(jnp.max(masked, axis=-1, keepdims=True))
        exps = jnp.exp(masked - biggest)
        probability = lower_precision(exps / lax.optimization_barrier(jnp.sum(exps, axis=-1, keepdims=True)))
        mixed = jnp.einsum('grqk,kgd->qgrd', probability, values, precision=lax.Precision.HIGHEST)
        return mixed.reshape(rows_per_block, QUERY_HEADS * HEAD_SIZE)
    outputs = lax.map(jax.checkpoint(block_attention), (query_block_list, position_blocks))
    return outputs.reshape(sequence_length, QUERY_HEADS * HEAD_SIZE)

def layer_forward(stream, weights, positions, rotary_angles):
    query_weight, key_matrix, value_matrix, out_weight, gate_weight, up_weight, down_weight, gain_one, gain_two = weights
    sequence_count, sequence_length, model_width = stream.shape
    normalized_rows = lower_precision(normalize(stream, gain_one))
    query_row_set = lower_precision(rotary_apply(lower_precision_backward(product_float32(normalized_rows, query_weight)).reshape(sequence_count, sequence_length, QUERY_HEADS, HEAD_SIZE), rotary_angles))
    key_row_set = lower_precision(rotary_apply(lower_precision_backward(product_float32(normalized_rows, key_matrix)).reshape(sequence_count, sequence_length, KEY_VALUE_HEADS, HEAD_SIZE), rotary_angles))
    value_row_set = lower_precision(lower_precision_backward(product_float32(normalized_rows, value_matrix))).reshape(sequence_count, sequence_length, KEY_VALUE_HEADS, HEAD_SIZE)
    attention_output = jax.vmap(lambda query_seq, key_seq, value_seq: attend(query_seq, key_seq, value_seq, positions))(query_row_set, key_row_set, value_row_set)
    attention_output = lower_precision(lower_precision_backward(attention_output))
    middle = stream + lower_precision_backward(product_float32(attention_output, out_weight))
    normed_two = lower_precision(normalize(middle, gain_two))
    gate_pre = lower_precision_backward(product_float32(normed_two, gate_weight))
    up_pre = lower_precision_backward(product_float32(normed_two, up_weight))
    hidden = lower_precision(gate_pre * jax.nn.sigmoid(gate_pre) * up_pre)
    return middle + lower_precision_backward(product_float32(hidden, down_weight))

def reference(tokens, pairing, cotangent, w_query, key_projection_weight, value_projection_weight, w_out, w_gate, w_up, w_down, attn_gain, ffn_gain):
    offsets = jnp.arange(BLK, dtype=jnp.int32)
    positions = (pairing[:, None] * BLK + offsets[None, :]).reshape(SEQLEN).astype(jnp.int32)
    rotary_angles = angles(positions)
    params = (w_query, key_projection_weight, value_projection_weight, w_out, w_gate, w_up, w_down, attn_gain, ffn_gain)
    params = tuple((param_array.astype(jnp.float32) for param_array in params))

    def forward(stream, weights):
        for layer_index in range(DECODER_LAYERS):
            stream = layer_forward(stream, tuple((param_array[layer_index] for param_array in weights)), positions, rotary_angles)
        return stream
    result, pullback = jax.vjp(forward, tokens.astype(jnp.float32), params)
    stream_grad, weight_grads = pullback(cotangent)
    return (result, stream_grad, weight_grads[0], weight_grads[1], weight_grads[2], weight_grads[3], weight_grads[4], weight_grads[5], weight_grads[6], weight_grads[7], weight_grads[8])
```

```python
import functools

import jax
import jax.numpy as jnp
from jax import lax
from jax.experimental import pallas as pl
from jax.experimental.pallas import tpu as pltpu
from jax.sharding import PartitionSpec as P

D = 576
HQ = 9
HK = 3
HD = 64
FF = 1536
BLK = 64
ROWS = 128
SEQ = 4096
KW = 192
CH = 256
EPS = 1e-05
BASE = 100000.0
NEG = -1e30
F32 = jnp.float32
BF = jnp.bfloat16
AXES = ("ctx", "fsdp")
OFFS = (0, -1, 1, 2)


def nn(a, b):
    return lax.dot_general(a, b, (((1,), (0,)), ((), ())), preferred_element_type=F32)


def nt(a, b):
    return lax.dot_general(a, b, (((1,), (1,)), ((), ())), preferred_element_type=F32)


def tn(a, b):
    return lax.dot_general(a, b, (((0,), (0,)), ((), ())), preferred_element_type=F32)


def pairs(move):
    found = []
    for z in range(4):
        for y in range(4):
            for c in range(2):
                for x in range(4):
                    a, b, e, f = move(z, y, c, x)
                    found.append(
                        (
                            ((z * 4 + y) * 2 + c) * 4 + x,
                            (((a % 4) * 4 + b % 4) * 2 + e) * 4 + f % 4,
                        )
                    )
    return found


def send(value, move):
    return lax.ppermute(value, AXES, pairs(move))


def plane(stage, k):
    def move(z, y, c, x):
        if (c + stage) % 2 == 0:
            return z, y + k, c, x
        return z + k, y, c, x

    return move


def along_x(k):
    return lambda z, y, c, x: (z, y, c, x + k)


def other_core(z, y, c, x):
    return z, y, 1 - c, x


def gather_stage(value, shift):
    return [value, send(value, shift(1)), send(value, shift(-1)), send(value, shift(2))]


def scatter_stage(parts, shift):
    return [
        parts[0],
        send(parts[1], shift(-1)),
        send(parts[2], shift(1)),
        send(parts[3], shift(2)),
    ]


def total(parts):
    return sum(p.astype(F32) for p in parts)


def gather_plane(value):
    first = jnp.concatenate(gather_stage(value, lambda k: plane(0, k)), 0)
    own = jnp.concatenate(gather_stage(first, lambda k: plane(1, k)), 0)
    return own, send(own, other_core)


def scatter_plane(own, other):
    both = total([own, send(other, other_core)]).astype(BF)
    parts = both.reshape((4, 512) + own.shape[1:])
    one = total(scatter_stage([parts[j] for j in range(4)], lambda k: plane(1, k))).astype(BF)
    one = one.reshape((4, 128) + own.shape[1:])
    return scatter_stage([one[j] for j in range(4)], lambda k: plane(0, k))


def reduce_all(own, other):
    half = total([own, send(other, other_core)]).astype(BF)
    part = total(scatter_stage([half[j] for j in range(4)], along_x)).astype(BF)
    part = total(gather_stage(part, lambda k: plane(0, k))).astype(BF)
    part = total(gather_stage(part, lambda k: plane(1, k))).astype(BF)
    return part, send(part, other_core)


def call(body, outs, args, smem=0, scratch=(), us=5.0, name=None):
    specs = [pl.BlockSpec(memory_space=pltpu.SMEM)] * smem
    specs += [pl.BlockSpec(memory_space=pltpu.VMEM)] * (len(args) - smem)
    return pl.pallas_call(
        body,
        out_shape=[jax.ShapeDtypeStruct(s, d) for s, d in outs],
        in_specs=specs,
        out_specs=[pl.BlockSpec(memory_space=pltpu.VMEM)] * len(outs),
        scratch_shapes=list(scratch),
        compiler_params=pltpu.CompilerParams(vmem_limit_bytes=58 * 1024 * 1024),
        cost_estimate=pl.CostEstimate(
            flops=int(us * 1.1e9), bytes_accessed=1000000, transcendentals=0
        ),
        name=name,
    )(*args)


def spin(v, cos, sin, back=False):
    lane = lax.broadcasted_iota(jnp.int32, (v.shape[0], 128), 1)
    low = (lane % 64) < 32
    pieces = []
    for j in range(v.shape[1] // 128):
        part = v[:, 128 * j : 128 * j + 128]
        swapped = jnp.where(low, pltpu.roll(part, 96, 1), pltpu.roll(part, 32, 1))
        if back:
            pieces.append(part * cos - swapped * sin)
        else:
            pieces.append(part * cos + swapped * sin)
    return jnp.concatenate(pieces, 1)


def rms(x):
    return lax.rsqrt(jnp.mean(x * x, axis=-1, keepdims=True) + EPS)


def norm_back(x, gain, grad):
    r = rms(x)
    inner = jnp.mean(grad * gain * x, axis=-1, keepdims=True)
    d_x = r * gain * grad - x * (r * r * r * inner)
    d_gain = jnp.sum(grad * x * r, axis=0, keepdims=True)
    return d_x, d_gain


def project(normed, weight, cos, sin, q_ref, kv_ref):
    mixed = nn(normed, weight)
    turned = spin(mixed[:, :768], cos, sin)
    q_ref[...] = (turned[:, :D].astype(BF).astype(F32) * (HD**-0.5)).astype(BF)
    kv_ref[:, :KW] = turned[:, D:768].astype(BF)
    kv_ref[:, KW:] = mixed[:, 768:960].astype(BF)


def first_kernel(x_ref, tok, p0, p1, p2, p3, cos, sin, normed, q, kv, w, gains, tmp):
    for j, piece in enumerate((p0, p1, p2, p3)):
        owner = lax.rem(x_ref[0] + (OFFS[j] + 4), 4)
        tmp[pl.ds(pl.multiple_of(owner * 144, 16), 144), :] = piece[...]
    w[...] = tmp[:, :960]
    g = tmp[:, 896:1024].astype(F32).T
    gains[...] = g[64:72, :]
    x = tok[...].astype(F32)
    n = (x * rms(x) * g[64:65, :]).astype(BF)
    normed[...] = n
    project(n, w[...], cos[...], sin[...], q, kv)


def spread(src, dst, block):
    dst[...] = jnp.zeros(dst.shape, BF)
    for h in range(HQ):
        g = h // 3
        dst[HD * h : HD * h + HD, HD * g : HD * g + HD] = src[
            BLK * block : BLK * block + BLK, HD * h : HD * h + HD
        ]


def allowed(chunk, position):
    key = lax.broadcasted_iota(jnp.int32, (CH, D), 0) + chunk * CH
    query = (lax.broadcasted_iota(jnp.int32, (CH, D), 1) % BLK) + position * BLK
    return key <= query


def attend_kernel(tab, own_pos, q, kvo, kvt, kp, vp, ot, lse, att, qbd, acc, stat):
    def place(s, carry):
        for base, ref in ((0, kvo), (32, kvt)):
            at = pl.ds(pl.multiple_of(tab[base + s] * BLK, BLK), BLK)
            rows = ref[pl.ds(pl.multiple_of(s * BLK, BLK), BLK), :]
            kp[at, :] = rows[:, :KW]
            vp[at, :] = rows[:, KW:]
        return carry

    lax.fori_loop(0, 32, place, 0)
    for block in range(2):
        position = own_pos[block]
        spread(q, qbd, block)
        stat[0:1, :] = jnp.full((1, D), NEG, F32)
        stat[1:2, :] = jnp.zeros((1, D), F32)
        acc[...] = jnp.zeros((KW, D), F32)

        def step(i, masked):
            at = pl.ds(pl.multiple_of(i * CH, CH), CH)
            s = nt(kp[at, :], qbd[...])
            if masked:
                s = jnp.where(allowed(i, position), s, NEG)
            old = stat[0:1, :]
            new = jnp.maximum(old, jnp.max(s, axis=0, keepdims=True))
            p = jnp.exp(s - new)
            fade = jnp.exp(old - new)
            stat[0:1, :] = new
            stat[1:2, :] = stat[1:2, :] * fade + jnp.sum(p, axis=0, keepdims=True)
            acc[...] = acc[...] * fade + tn(vp[at, :], p.astype(BF))

        def loop(i, carry):
            step(i, False)
            return carry

        last = position // 4
        lax.fori_loop(0, last, loop, 0)
        step(last, True)
        result = acc[...] / stat[1:2, :]
        ot[block] = result
        lse[block] = jnp.broadcast_to(stat[0:1, :] + jnp.log(stat[1:2, :]), (8, D))
        turned = result.T
        for h in range(HQ):
            g = h // 3
            att[BLK * block : BLK * block + BLK, HD * h : HD * h + HD] = turned[
                HD * h : HD * h + HD, HD * g : HD * g + HD
            ].astype(BF)


def ffn_forward(n2, pieces):
    out = None
    for p in pieces:
        gate = nt(n2, p[0:KW, :])
        up = nt(n2, p[KW : 2 * KW, :])
        hidden = (gate * jax.nn.sigmoid(gate) * up).astype(BF)
        term = nn(hidden, p[2 * KW : 3 * KW, :])
        out = term if out is None else out + term
    return out


def middle_kernel(stream, att, wo, gains, gain_row, w0, w1, w2, w3, v0, v1, v2, v3, *rest):
    if len(rest) > 3:
        wqkv, cos, sin, middle_ref, n2_ref, out, normed, q, kv = rest
    else:
        middle_ref, n2_ref, out = rest
    middle = stream[...].astype(F32) + nn(att[...], wo[...])
    middle_ref[...] = middle
    n2 = (middle * rms(middle) * gains[gain_row + 1 : gain_row + 2, :]).astype(BF)
    n2_ref[...] = n2
    result = middle + ffn_forward(n2, (w0, w1, w2, w3, v0, v1, v2, v3))
    out[...] = result
    if len(rest) > 3:
        n = (result * rms(result) * gains[gain_row + 2 : gain_row + 3, :]).astype(BF)
        normed[...] = n
        project(n, wqkv[...], cos[...], sin[...], q, kv)


def ffn_back_kernel(
    gain_row, grad, middle, n2_ref, att, wo, gains, w0, w1, w2, w3, v0, v1, v2, v3,
    g_own, g_oth, mid_grad, d_out, d_wo, d_gain,
):
    g = grad[...]
    branch = g.astype(BF)
    n2 = n2_ref[...]
    n2_grad = None
    for j, p in enumerate((w0, w1, w2, w3, v0, v1, v2, v3)):
        dst = g_own if j < 4 else g_oth
        k = j % 4
        gate = nt(n2, p[0:KW, :])
        up = nt(n2, p[KW : 2 * KW, :])
        s = jax.nn.sigmoid(gate)
        hidden = (gate * s * up).astype(BF)
        hidden_grad = nt(branch, p[2 * KW : 3 * KW, :])
        gate_grad = (hidden_grad * up * s * (1.0 + gate * (1.0 - s))).astype(BF)
        up_grad = (hidden_grad * gate * s).astype(BF)
        dst[k, 0:KW, :] = tn(gate_grad, n2).astype(BF)
        dst[k, KW : 2 * KW, :] = tn(up_grad, n2).astype(BF)
        dst[k, 2 * KW : 3 * KW, :] = tn(hidden, branch).astype(BF)
        term = nn(gate_grad, p[0:KW, :]) + nn(up_grad, p[KW : 2 * KW, :])
        n2_grad = term if n2_grad is None else n2_grad + term
    part, gain_grad = norm_back(middle[...], gains[gain_row + 1 : gain_row + 2, :], n2_grad)
    m_grad = g + part
    mid_grad[...] = m_grad
    d_gain[...] = jnp.broadcast_to(gain_grad, (8, D))
    ab = m_grad.astype(BF)
    d_wo[...] = tn(att[...], ab).astype(BF)
    d_out[...] = nt(ab, wo[...]).astype(BF)


def attend_back_kernel(
    tab, own_pos, q, d_out, kp, vp, ot, lse, cos, sin, dkv_own, dkv_oth, dq_pre,
    qbd, dbd, dk, dv, dqt, flat,
):
    dk[...] = jnp.zeros(dk.shape, F32)
    dv[...] = jnp.zeros(dv.shape, F32)
    flat[:, D:] = jnp.zeros((ROWS, 64), F32)
    for block in range(2):
        position = own_pos[block]
        spread(q, qbd, block)
        spread(d_out, dbd, block)
        delta = jnp.sum(ot[block] * dbd[...].astype(F32).T, axis=0, keepdims=True)
        log_total = lse[block][0:1, :]
        dqt[...] = jnp.zeros((KW, D), F32)

        def step(i, masked):
            at = pl.ds(pl.multiple_of(i * CH, CH), CH)
            p = jnp.exp(nt(kp[at, :], qbd[...]) - log_total)
            if masked:
                p = jnp.where(allowed(i, position), p, 0.0)
            p_grad = nt(vp[at, :], dbd[...])
            s_grad = (p * (p_grad - delta)).astype(BF)
            dv[at, :] += nn(p.astype(BF), dbd[...])
            dk[at, :] += nn(s_grad, qbd[...])
            dqt[...] += tn(kp[at, :], s_grad)

        def loop(i, carry):
            step(i, False)
            return carry

        last = position // 4
        lax.fori_loop(0, last, loop, 0)
        step(last, True)
        turned = (dqt[...] * (HD**-0.5)).T
        for h in range(HQ):
            g = h // 3
            flat[BLK * block : BLK * block + BLK, HD * h : HD * h + HD] = turned[
                HD * h : HD * h + HD, HD * g : HD * g + HD
            ]
    dq_pre[...] = spin(flat[...], cos[...], sin[...], True)[:, :D].astype(BF)

    def place(s, carry):
        for base, ref in ((0, dkv_own), (32, dkv_oth)):
            at = pl.ds(pl.multiple_of(tab[base + s] * BLK, BLK), BLK)
            to = pl.ds(pl.multiple_of(s * BLK, BLK), BLK)
            ref[to, :] = jnp.concatenate([dk[at, :].astype(BF), dv[at, :].astype(BF)], 1)
        return carry

    lax.fori_loop(0, 32, place, 0)


def project_back_kernel(
    gain_row, place_ref, t0, t1, t2, t3, dq_pre, normed, stream, gains, wqkv, mid_grad,
    d_wo, d_gain_two, cos, sin, grad, g_own, g_oth, kbuf, full,
):
    x, c = place_ref[0], place_ref[1]
    dkv = t0[...].astype(F32) + t1[...].astype(F32) + t2[...].astype(F32) + t3[...].astype(F32)
    kbuf[:, :KW] = dkv[:, :KW]
    kbuf[:, KW:] = jnp.zeros((ROWS, 64), F32)
    dk_pre = spin(kbuf[...], cos[...], sin[...], True)[:, :KW].astype(BF)
    dqk = jnp.concatenate([dq_pre[...], dk_pre], 1)
    dv_pre = dkv[:, KW:].astype(BF)
    n = normed[...]
    full[0, :D, :] = tn(n, dqk).astype(BF)
    full[1, :D, :] = jnp.concatenate([tn(n, dv_pre).astype(BF), d_wo[...]], 1)
    n_grad = nt(jnp.concatenate([dqk, dv_pre], 1), wqkv[...])
    part, gain_grad = norm_back(stream[...].astype(F32), gains[gain_row : gain_row + 1, :], n_grad)
    grad[...] = mid_grad[...] + part
    full[0, D:, :] = jnp.zeros((16, 768), BF)
    full[1, D:, :] = jnp.zeros((16, 768), BF)
    full[0, D:, :D] = jnp.broadcast_to(gain_grad, (16, D)).astype(BF)
    full[1, D:, :D] = jnp.broadcast_to(d_gain_two[0:1, :], (16, D)).astype(BF)
    for j in range(4):
        owner = lax.rem(x + (OFFS[j] + 4), 4)
        at = pl.ds(pl.multiple_of(owner * 144, 16), 144)
        g_own[j, :144, :] = full[c, at, :]
        g_own[j, 144:, :] = full[c, D:, :]
        g_oth[j, :144, :] = full[1 - c, at, :]
        g_oth[j, 144:, :] = full[1 - c, D:, :]


def local(tokens, pairing, cotangent, w_query, w_key, w_value, w_out, w_gate, w_up, w_down, attn_gain, ffn_gain):
    ctx = lax.axis_index("ctx")
    x = lax.axis_index("fsdp")
    z, y, c = ctx // 8, (ctx // 2) % 4, ctx % 2

    gains_in = jnp.stack([attn_gain[0], ffn_gain[0], attn_gain[1], ffn_gain[1]], 1)
    bundle = jnp.concatenate(
        [w_query[0], w_key[0], w_value[0], gains_in, jnp.zeros((144, 60), BF)], 1
    )
    first_pieces = gather_stage(bundle, along_x)
    rest = jnp.concatenate([w_out[0], w_query[1], w_key[1], w_value[1], w_out[1]], 1)
    rest = lax.all_gather(rest, "fsdp", axis=0, tiled=True)
    wo = [rest[:, :D], rest[:, D + 960 :]]

    def halves(layer):
        parts = [
            lax.dynamic_slice_in_dim(m, KW * c, KW, 0)
            for m in (w_gate[layer].T, w_up[layer].T, w_down[layer])
        ]
        return jnp.concatenate(parts, 0)

    ffn = []
    for layer in range(2):
        own = gather_stage(halves(layer), along_x)
        ffn.append(own + [send(p, other_core) for p in own])

    spot = jnp.arange(16, dtype=jnp.int32)
    step = jnp.array(OFFS, jnp.int32)
    inner, outer = step[spot % 4], step[spot // 4]

    def owners(core):
        along_y = jnp.where(core == 0, inner, outer)
        along_z = jnp.where(core == 0, outer, inner)
        return ((z + along_z) % 4) * 8 + ((y + along_y) % 4) * 2 + core

    owner = jnp.concatenate([owners(c), owners(1 - c)])
    tab = pairing.reshape(32, 2)[owner].reshape(64)
    own_pos = lax.dynamic_slice_in_dim(pairing, 2 * ctx, 2)
    rows = (own_pos[:, None] * BLK + jnp.arange(BLK, dtype=jnp.int32)[None, :]).reshape(ROWS)
    frequency = BASE ** (-(jnp.arange(HD // 2, dtype=F32) * 2.0 / HD))
    angle = rows.astype(F32)[:, None] * frequency[None, :]
    cos1, sin1 = jnp.cos(angle), jnp.sin(angle)
    cos = jnp.concatenate([cos1] * 4, 1)
    sin = jnp.concatenate([-sin1, sin1] * 2, 1)
    place = jnp.stack([x, c]).astype(jnp.int32)

    act = (ROWS, D)
    stream0 = tokens[0]
    normed0, q0, kv0, wqkv0, gains = call(
        first_kernel,
        [(act, BF), (act, BF), ((ROWS, 384), BF), ((D, 960), BF), ((8, D), F32)],
        [place, stream0, *first_pieces, cos, sin],
        smem=1,
        scratch=[pltpu.VMEM((D, 1024), BF)],
        us=3.0,
        name="project_first",
    )

    def attend(q, kv):
        own, oth = gather_plane(kv)
        return call(
            attend_kernel,
            [
                ((SEQ, KW), BF),
                ((SEQ, KW), BF),
                ((2, KW, D), F32),
                ((2, 8, D), F32),
                (act, BF),
            ],
            [tab, own_pos, q, own, oth],
            smem=2,
            scratch=[pltpu.VMEM((D, KW), BF), pltpu.VMEM((KW, D), F32), pltpu.VMEM((8, D), F32)],
            us=12.0,
            name="attend",
        )

    kp0, vp0, ot0, lse0, att0 = attend(q0, kv0)
    wqkv1 = rest[:, D : D + 960]
    middle0, n20, stream1, normed1, q1, kv1 = call(
        lambda s, a, o, g, *r: middle_kernel(s, a, o, g, 0, *r),
        [(act, F32), (act, BF), (act, F32), (act, BF), (act, BF), ((ROWS, 384), BF)],
        [stream0, att0, wo[0], gains, *ffn[0], wqkv1, cos, sin],
        us=8.0,
        name="middle_first",
    )
    kp1, vp1, ot1, lse1, att1 = attend(q1, kv1)
    middle1, n21, out = call(
        lambda s, a, o, g, *r: middle_kernel(s, a, o, g, 2, *r),
        [(act, F32), (act, BF), (act, F32)],
        [stream1, att1, wo[1], gains, *ffn[1]],
        us=6.0,
        name="middle_last",
    )

    def back(layer, grad, middle, n2, att, q, kp, vp, ot, lse, normed, stream, wqkv):
        g_own, g_oth, mid_grad, d_out, d_wo, d_gain_two = call(
            functools.partial(ffn_back_kernel, 2 * layer),
            [
                ((4, D, D), BF),
                ((4, D, D), BF),
                (act, F32),
                (act, BF),
                ((D, D), BF),
                ((8, D), F32),
            ],
            [grad, middle, n2, att, wo[layer], gains, *ffn[layer]],
            us=10.0,
            name="ffn_back",
        )
        ffn_sums = reduce_all(g_own, g_oth)
        dkv_own, dkv_oth, dq_pre = call(
            attend_back_kernel,
            [((2048, 384), BF), ((2048, 384), BF), (act, BF)],
            [tab, own_pos, q, d_out, kp, vp, ot, lse, cos, sin],
            smem=2,
            scratch=[
                pltpu.VMEM((D, KW), BF),
                pltpu.VMEM((D, KW), BF),
                pltpu.VMEM((SEQ, KW), F32),
                pltpu.VMEM((SEQ, KW), F32),
                pltpu.VMEM((KW, D), F32),
                pltpu.VMEM((ROWS, 640), F32),
            ],
            us=20.0,
            name="attend_back",
        )
        terms = scatter_plane(dkv_own, dkv_oth)
        new_grad, a_own, a_oth = call(
            functools.partial(project_back_kernel, 2 * layer),
            [(act, F32), ((4, 160, 768), BF), ((4, 160, 768), BF)],
            [place, *terms, dq_pre, normed, stream, gains, wqkv, mid_grad, d_wo, d_gain_two, cos, sin],
            smem=1,
            scratch=[pltpu.VMEM((ROWS, 256), F32), pltpu.VMEM((2, D + 16, 768), BF)],
            us=5.0,
            name="project_back",
        )
        attn_sums = reduce_all(a_own, a_oth)
        return new_grad, ffn_sums, attn_sums

    grad1, ffn1, attn1 = back(
        1, cotangent[0], middle1, n21, att1, q1, kp1, vp1, ot1, lse1, normed1, stream1, wqkv1
    )
    grad0, ffn0, attn0 = back(
        0, grad1, middle0, n20, att0, q0, kp0, vp0, ot0, lse0, normed0, stream0, wqkv0
    )

    def ordered(sums):
        mine, theirs = (s.astype(F32) for s in sums)
        return jnp.where(c == 0, mine, theirs), jnp.where(c == 0, theirs, mine)

    results = []
    for ffn_sums, attn_sums in ((ffn0, attn0), (ffn1, attn1)):
        low, high = ordered(ffn_sums)
        both = jnp.concatenate([low.reshape(3, KW, D), high.reshape(3, KW, D)], 1)
        one, two = ordered(attn_sums)
        gain_at = lambda v: lax.dynamic_slice_in_dim(v[144, :D], 144 * x, 144, 0)
        results.append(
            (
                one[:144, :D],
                one[:144, D:],
                two[:144, :KW],
                two[:144, KW:],
                both[0].T,
                both[1].T,
                both[2],
                gain_at(one),
                gain_at(two),
            )
        )
    stacked = [jnp.stack([results[0][i], results[1][i]]) for i in range(9)]
    return (out[None], grad0[None], *stacked)


def solution(mesh):
    rows = P("fsdp", "ctx", None)
    wide = P(None, "fsdp", None)
    deep = P(None, None, "fsdp")
    flat = P(None, "fsdp")
    return jax.shard_map(
        local,
        mesh=mesh,
        in_specs=(rows, P(), rows, wide, wide, wide, wide, deep, deep, wide, flat, flat),
        out_specs=(rows, rows, wide, wide, wide, wide, deep, deep, wide, flat, flat),
        check_vma=False,
    )
```

```python
import functools

import jax
import jax.numpy as jnp
from jax import lax
from jax.experimental import pallas as pl
from jax.experimental.pallas import tpu as pltpu
from jax.sharding import PartitionSpec as P

D = 576
HQ = 9
HK = 3
HD = 64
FF = 1536
BLK = 64
ROWS = 128
SEQ = 4096
KW = 192
CH = 256
EPS = 1e-05
BASE = 100000.0
NEG = -1e30
F32 = jnp.float32
BF = jnp.bfloat16
AXES = ("ctx", "fsdp")
OFFS = (0, -1, 1, 2)
PACK = 2 * D + 2 * 224


def nn(a, b):
    return lax.dot_general(a, b, (((1,), (0,)), ((), ())), preferred_element_type=F32)


def nt(a, b):
    return lax.dot_general(a, b, (((1,), (1,)), ((), ())), preferred_element_type=F32)


def tn(a, b):
    return lax.dot_general(a, b, (((0,), (0,)), ((), ())), preferred_element_type=F32)


def pairs(move):
    found = []
    for z in range(4):
        for y in range(4):
            for c in range(2):
                for x in range(4):
                    a, b, e, f = move(z, y, c, x)
                    found.append(
                        (
                            ((z * 4 + y) * 2 + c) * 4 + x,
                            (((a % 4) * 4 + b % 4) * 2 + e) * 4 + f % 4,
                        )
                    )
    return found


def send(value, move):
    return lax.ppermute(value, AXES, pairs(move))


def plane(stage, k):
    def move(z, y, c, x):
        if (c + stage) % 2 == 0:
            return z, y + k, c, x
        return z + k, y, c, x

    return move


def along_x(k):
    return lambda z, y, c, x: (z, y, c, x + k)


def other_core(z, y, c, x):
    return z, y, 1 - c, x


def gather_stage(value, shift):
    return [value, send(value, shift(1)), send(value, shift(-1)), send(value, shift(2))]


def scatter_stage(parts, shift):
    return [
        parts[0],
        send(parts[1], shift(-1)),
        send(parts[2], shift(1)),
        send(parts[3], shift(2)),
    ]


def after(value, *others):
    return lax.optimization_barrier((value, *others))[0]


def total(parts):
    return sum(p.astype(F32) for p in parts)


def plane_one(k):
    return plane(0, k)


def plane_two(k):
    return plane(1, k)


def swap(values):
    return [send(v, other_core) for v in values]


def gather_plane(value):
    first = jnp.concatenate(gather_stage(value, plane_one), 0)
    own = gather_stage(first, plane_two)
    return own + swap(own), first


def scatter_plane(own, other, waits=()):
    both = total([own, send(other, other_core)]).astype(BF)
    parts = both.reshape((4, 512) + own.shape[1:])
    one = total(scatter_stage([parts[j] for j in range(4)], plane_two)).astype(BF)
    one = after(one, *waits).reshape((4, 128) + own.shape[1:])
    return scatter_stage([one[j] for j in range(4)], plane_one)


def add_cores(own, other):
    return total([own, send(other, other_core)]).astype(BF)


def call(body, outs, args, smem=0, scratch=(), us=5.0, name=None):
    specs = [pl.BlockSpec(memory_space=pltpu.SMEM)] * smem
    specs += [pl.BlockSpec(memory_space=pltpu.VMEM)] * (len(args) - smem)
    return pl.pallas_call(
        body,
        out_shape=[jax.ShapeDtypeStruct(s, d) for s, d in outs],
        in_specs=specs,
        out_specs=[pl.BlockSpec(memory_space=pltpu.VMEM)] * len(outs),
        scratch_shapes=list(scratch),
        compiler_params=pltpu.CompilerParams(vmem_limit_bytes=58 * 1024 * 1024),
        cost_estimate=pl.CostEstimate(
            flops=int(us * 1.1e9), bytes_accessed=1000000, transcendentals=0
        ),
        name=name,
    )(*args)


def spin(v, cos, sin, back=False):
    lane = lax.broadcasted_iota(jnp.int32, (v.shape[0], 128), 1)
    low = (lane % 64) < 32
    pieces = []
    for j in range(v.shape[1] // 128):
        part = v[:, 128 * j : 128 * j + 128]
        swapped = jnp.where(low, pltpu.roll(part, 96, 1), pltpu.roll(part, 32, 1))
        if back:
            pieces.append(part * cos - swapped * sin)
        else:
            pieces.append(part * cos + swapped * sin)
    return jnp.concatenate(pieces, 1)


def rms(x):
    return lax.rsqrt(jnp.mean(x * x, axis=-1, keepdims=True) + EPS)


def norm_back(x, gain, grad):
    r = rms(x)
    inner = jnp.mean(grad * gain * x, axis=-1, keepdims=True)
    d_x = r * gain * grad - x * (r * r * r * inner)
    d_gain = jnp.sum(grad * x * r, axis=0, keepdims=True)
    return d_x, d_gain


def project(normed, weight, cos, sin, q_ref, kv_ref):
    mixed = nn(normed, weight)
    turned = spin(mixed[:, :768], cos, sin)
    q_ref[...] = (turned[:, :D].astype(BF).astype(F32) * (HD**-0.5)).astype(BF)
    kv_ref[:, :KW] = turned[:, D:768].astype(BF)
    kv_ref[:, KW:] = mixed[:, 768:960].astype(BF)


def first_kernel(x_ref, tok, p0, p1, p2, p3, cos, sin, normed, q, kv, w, gains, tmp):
    for j, piece in enumerate((p0, p1, p2, p3)):
        owner = lax.rem(x_ref[0] + (OFFS[j] + 4), 4)
        tmp[pl.ds(pl.multiple_of(owner * 144, 16), 144), :] = piece[...]
    w[...] = tmp[:, :960]
    g = tmp[:, 896:1024].astype(F32).T
    gains[...] = g[64:72, :]
    x = tok[...].astype(F32)
    n = (x * rms(x) * g[64:65, :]).astype(BF)
    normed[...] = n
    project(n, w[...], cos[...], sin[...], q, kv)


def spread(src, dst, block):
    dst[...] = jnp.zeros(dst.shape, BF)
    for h in range(HQ):
        g = h // 3
        dst[HD * h : HD * h + HD, HD * g : HD * g + HD] = src[
            BLK * block : BLK * block + BLK, HD * h : HD * h + HD
        ]


def allowed(chunk, position):
    key = lax.broadcasted_iota(jnp.int32, (CH, D), 0) + chunk * CH
    query = (lax.broadcasted_iota(jnp.int32, (CH, D), 1) % BLK) + position * BLK
    return key <= query


def attend_kernel(tab, own_pos, q, *rest):
    kv, (kp, vp, ot, lse, att, qbd, acc, stat) = rest[:8], rest[8:]

    def place(s, carry):
        for j, ref in enumerate(kv):
            at = pl.ds(pl.multiple_of(tab[8 * j + s] * BLK, BLK), BLK)
            rows = ref[pl.ds(pl.multiple_of(s * BLK, BLK), BLK), :]
            kp[at, :] = rows[:, :KW]
            vp[at, :] = rows[:, KW:]
        return carry

    lax.fori_loop(0, 8, place, 0)
    for block in range(2):
        position = own_pos[block]
        spread(q, qbd, block)
        stat[0:1, :] = jnp.full((1, D), NEG, F32)
        stat[1:2, :] = jnp.zeros((1, D), F32)
        acc[...] = jnp.zeros((KW, D), F32)

        def step(i, masked):
            at = pl.ds(pl.multiple_of(i * CH, CH), CH)
            s = nt(kp[at, :], qbd[...])
            if masked:
                s = jnp.where(allowed(i, position), s, NEG)
            old = stat[0:1, :]
            new = jnp.maximum(old, jnp.max(s, axis=0, keepdims=True))
            p = jnp.exp(s - new)
            fade = jnp.exp(old - new)
            stat[0:1, :] = new
            stat[1:2, :] = stat[1:2, :] * fade + jnp.sum(p, axis=0, keepdims=True)
            acc[...] = acc[...] * fade + tn(vp[at, :], p.astype(BF))

        def loop(i, carry):
            step(i, False)
            return carry

        last = position // 4
        lax.fori_loop(0, last, loop, 0)
        step(last, True)
        result = acc[...] / stat[1:2, :]
        ot[block] = result
        lse[block] = jnp.broadcast_to(stat[0:1, :] + jnp.log(stat[1:2, :]), (8, D))
        turned = result.T
        for h in range(HQ):
            g = h // 3
            att[BLK * block : BLK * block + BLK, HD * h : HD * h + HD] = turned[
                HD * h : HD * h + HD, HD * g : HD * g + HD
            ].astype(BF)


def ffn_forward(n2, pieces):
    out = None
    for ref in pieces:
        for k in range(4):
            gate = nt(n2, ref[k, 0:KW, :])
            up = nt(n2, ref[k, KW : 2 * KW, :])
            hidden = (gate * jax.nn.sigmoid(gate) * up).astype(BF)
            term = nn(hidden, ref[k, 2 * KW : 3 * KW, :])
            out = term if out is None else out + term
    return out


def middle_first_kernel(
    place, stream, att, gains, w, v, r0, r1, r2, r3, s0, s1, s2, s3, cos, sin,
    middle_ref, n2_ref, out, normed, q, kv, wo0, wqkv1, wo1,
):
    x, c = place[0], place[1]

    def sort(outs, projections):
        for j in range(4):
            owner = lax.rem(x + (OFFS[j] + 4), 4)
            at = pl.ds(pl.multiple_of(owner * 144, 16), 144)
            wo0[at, :] = outs[j][:, :D]
            wo1[at, :] = outs[j][:, D:]
            wqkv1[at, :] = projections[j][:, :960]

    @pl.when(c == 0)
    def _():
        sort((r0, r1, r2, r3), (s0, s1, s2, s3))

    @pl.when(c == 1)
    def _():
        sort((s0, s1, s2, s3), (r0, r1, r2, r3))

    middle = stream[...].astype(F32) + nn(att[...], wo0[...])
    middle_ref[...] = middle
    n2 = (middle * rms(middle) * gains[1:2, :]).astype(BF)
    n2_ref[...] = n2
    result = middle + ffn_forward(n2, (w, v))
    out[...] = result
    n = (result * rms(result) * gains[2:3, :]).astype(BF)
    normed[...] = n
    project(n, wqkv1[...], cos[...], sin[...], q, kv)


def middle_last_kernel(stream, att, wo, gains, w, v, middle_ref, n2_ref, out):
    middle = stream[...] + nn(att[...], wo[...])
    middle_ref[...] = middle
    n2 = (middle * rms(middle) * gains[3:4, :]).astype(BF)
    n2_ref[...] = n2
    out[...] = (middle + ffn_forward(n2, (w, v))).T


def ffn_grads(branch, n2, weights, dst):
    n2_grad = None
    for k in range(4):
        p = weights.at[k]
        gate = nt(n2, p[0:KW, :])
        up = nt(n2, p[KW : 2 * KW, :])
        s = jax.nn.sigmoid(gate)
        hidden = (gate * s * up).astype(BF)
        hidden_grad = nt(branch, p[2 * KW : 3 * KW, :])
        gate_grad = (hidden_grad * up * s * (1.0 + gate * (1.0 - s))).astype(BF)
        up_grad = (hidden_grad * gate * s).astype(BF)
        dst[k, 0:KW, :] = tn(gate_grad, n2).astype(BF)
        dst[k, KW : 2 * KW, :] = tn(up_grad, n2).astype(BF)
        dst[k, 2 * KW : 3 * KW, :] = tn(hidden, branch).astype(BF)
        term = nn(gate_grad, p[0:KW, :]) + nn(up_grad, p[KW : 2 * KW, :])
        n2_grad = term if n2_grad is None else n2_grad + term
    return n2_grad


def ffn_back_other_kernel(grad, n2, v, g_oth, part):
    part[...] = ffn_grads(grad[...].astype(BF), n2[...], v, g_oth)


def ffn_back_own_kernel(
    gain_row, grad, n2, w, half_grad, middle, att, wo, gains, g_own, mid_grad, d_out, d_wo, d_gain
):
    g = grad[...]
    n2_grad = half_grad[...] + ffn_grads(g.astype(BF), n2[...], w, g_own)
    part, gain_grad = norm_back(middle[...], gains[gain_row + 1 : gain_row + 2, :], n2_grad)
    m_grad = g + part
    mid_grad[...] = m_grad
    d_gain[...] = jnp.broadcast_to(gain_grad, (8, D))
    ab = m_grad.astype(BF)
    d_wo[...] = tn(att[...], ab).astype(BF)
    d_out[...] = nt(ab, wo[...]).astype(BF)


def attend_back_kernel(
    tab, own_pos, q, d_out, kp, vp, ot, lse, cos, sin, dkv_own, dkv_oth, dq_pre,
    qbd, dbd, dk, dv, dqt, flat,
):
    dk[...] = jnp.zeros(dk.shape, F32)
    dv[...] = jnp.zeros(dv.shape, F32)
    flat[:, D:] = jnp.zeros((ROWS, 64), F32)
    for block in range(2):
        position = own_pos[block]
        spread(q, qbd, block)
        spread(d_out, dbd, block)
        delta = jnp.sum(ot[block] * dbd[...].astype(F32).T, axis=0, keepdims=True)
        log_total = lse[block][0:1, :]
        dqt[...] = jnp.zeros((KW, D), F32)

        def step(i, masked):
            at = pl.ds(pl.multiple_of(i * CH, CH), CH)
            p = jnp.exp(nt(kp[at, :], qbd[...]) - log_total)
            if masked:
                p = jnp.where(allowed(i, position), p, 0.0)
            p_grad = nt(vp[at, :], dbd[...])
            s_grad = (p * (p_grad - delta)).astype(BF)
            dv[at, :] += nn(p.astype(BF), dbd[...])
            dk[at, :] += nn(s_grad, qbd[...])
            dqt[...] += tn(kp[at, :], s_grad)

        def loop(i, carry):
            step(i, False)
            return carry

        last = position // 4
        lax.fori_loop(0, last, loop, 0)
        step(last, True)
        turned = (dqt[...] * (HD**-0.5)).T
        for h in range(HQ):
            g = h // 3
            flat[BLK * block : BLK * block + BLK, HD * h : HD * h + HD] = turned[
                HD * h : HD * h + HD, HD * g : HD * g + HD
            ]
    dq_pre[...] = spin(flat[...], cos[...], sin[...], True)[:, :D].astype(BF)

    def place(s, carry):
        for base, ref in ((0, dkv_own), (32, dkv_oth)):
            at = pl.ds(pl.multiple_of(tab[base + s] * BLK, BLK), BLK)
            to = pl.ds(pl.multiple_of(s * BLK, BLK), BLK)
            ref[to, :] = jnp.concatenate([dk[at, :].astype(BF), dv[at, :].astype(BF)], 1)
        return carry

    lax.fori_loop(0, 32, place, 0)


def project_back_kernel(
    gain_row, place_ref, t0, t1, t2, t3, dq_pre, normed, stream, gains, wqkv, mid_grad,
    d_wo, d_gain_two, cos, sin, grad, g_own, g_oth, kbuf, full, side,
):
    x, c = place_ref[0], place_ref[1]
    dkv = t0[...].astype(F32) + t1[...].astype(F32) + t2[...].astype(F32) + t3[...].astype(F32)
    kbuf[:, :KW] = dkv[:, :KW]
    kbuf[:, KW:] = jnp.zeros((ROWS, 64), F32)
    dk_pre = spin(kbuf[...], cos[...], sin[...], True)[:, :KW].astype(BF)
    dqk = jnp.concatenate([dq_pre[...], dk_pre], 1)
    dv_pre = dkv[:, KW:].astype(BF)
    n = normed[...]
    full[0] = tn(n, dq_pre[...]).astype(BF)
    full[1] = d_wo[...]
    side[:, : 2 * KW] = tn(n, jnp.concatenate([dk_pre, dv_pre], 1)).astype(BF)
    side[:, 2 * KW :] = jnp.zeros((D, KW), BF)
    n_grad = nt(jnp.concatenate([dqk, dv_pre], 1), wqkv[...])
    part, gain_grad = norm_back(stream[...].astype(F32), gains[gain_row : gain_row + 1, :], n_grad)
    total_grad = mid_grad[...] + part
    grad[...] = total_grad.T if grad.shape[0] == D else total_grad
    row = lax.broadcasted_iota(jnp.int32, (16, D), 0)
    both_gains = jnp.where(row == 0, gain_grad, d_gain_two[0:1, :]).astype(BF)

    def write(low, high):
        for j in range(4):
            start = pl.multiple_of(lax.rem(x + (OFFS[j] + 4), 4) * 144, 16)
            low[j, :144, :] = full[0, pl.ds(start, 144), :]
            high[j, :144, :] = full[1, pl.ds(start, 144), :]
            low[j, 144:, :] = side[pl.ds(start, 80), :]
            high[j, 144:208, :] = side[pl.ds(start + 80, 64), :]
            high[j, 208:, :] = both_gains

    @pl.when(c == 0)
    def _():
        write(g_own, g_oth)

    @pl.when(c == 1)
    def _():
        write(g_oth, g_own)


def pack_kernel(place, *refs):
    outs, tmp = refs[16:20], refs[20]
    at = 0
    for k, rows in enumerate((D, D, 224, 224)):
        shares = refs[4 * k : 4 * k + 4]
        tmp[at : at + rows, :] = sum(r[...].astype(F32) for r in shares).astype(BF)
        at += rows
    for j in range(4):
        start = lax.rem(place[2] + (OFFS[j] + 4), 4) * (PACK // 4)
        outs[j][...] = tmp[pl.ds(pl.multiple_of(start, 16), PACK // 4), :]


def unpack_kernel(
    place, m0, m1, m2, m3, t0, t1, t2, t3,
    dq, dk, dv, do, dg, du, dd, gains, mine, theirs, turn,
):
    c = place[1]
    for j in range(4):
        start = lax.rem(place[2] + (OFFS[j] + 4), 4) * (PACK // 4)
        mine[pl.ds(pl.multiple_of(start, 16), PACK // 4), :] = (m0, m1, m2, m3)[j][...]
        start = lax.rem(place[3] + (OFFS[j] + 4), 4) * (PACK // 4)
        theirs[pl.ds(pl.multiple_of(start, 16), PACK // 4), :] = (t0, t1, t2, t3)[j][...]
    for layer in range(2):
        a, b = mine.at[D * layer : D * layer + D], theirs.at[D * layer : D * layer + D]
        at_a = pl.ds(pl.multiple_of(c * KW, 64), KW)
        at_b = pl.ds(pl.multiple_of((1 - c) * KW, 64), KW)
        for k, ref in enumerate((dg, du, dd)):
            turn[at_a, :] = a[KW * k : KW * k + KW, :].astype(F32)
            turn[at_b, :] = b[KW * k : KW * k + KW, :].astype(F32)
            ref[layer] = turn[...].T

    def write(low, high):
        for layer in range(2):
            at = 2 * D + 224 * layer
            dq[layer] = low[at : at + 144, :].astype(F32)
            do[layer] = high[at : at + 144, :].astype(F32)
            for ref, lanes in ((dk, slice(0, KW)), (dv, slice(KW, 2 * KW))):
                ref[layer, :80, :] = low[at + 144 : at + 224, lanes].astype(F32)
                ref[layer, 80:, :] = high[at + 144 : at + 208, lanes].astype(F32)
            gains[8 * layer : 8 * layer + 8, :] = high[at + 208 : at + 224, :].astype(F32)[:8, :]

    @pl.when(c == 0)
    def _():
        write(mine, theirs)

    @pl.when(c == 1)
    def _():
        write(theirs, mine)


def local(tokens, pairing, cotangent, w_query, w_key, w_value, w_out, w_gate, w_up, w_down, attn_gain, ffn_gain):
    ctx = lax.axis_index("ctx")
    x = lax.axis_index("fsdp")
    z, y, c = ctx // 8, (ctx // 2) % 4, ctx % 2

    gains_in = jnp.stack([attn_gain[0], ffn_gain[0], attn_gain[1], ffn_gain[1]], 1)
    bundle = jnp.concatenate(
        [w_query[0], w_key[0], w_value[0], gains_in, jnp.zeros((144, 60), BF)], 1
    )
    first_pieces = gather_stage(bundle, along_x)
    outs = jnp.concatenate([w_out[0], w_out[1]], 1)
    later = jnp.concatenate([w_query[1], w_key[1], w_value[1], jnp.zeros((144, KW), BF)], 1)
    rest = gather_stage(jnp.where(c == 0, outs, later), along_x)

    def halves(layer):
        parts = [
            lax.dynamic_slice_in_dim(m, KW * c, KW, 0)
            for m in (w_gate[layer].T, w_up[layer].T, w_down[layer])
        ]
        return jnp.concatenate(parts, 0)

    def gather_ffn(mine):
        return lax.all_gather(mine, "fsdp", axis=0)

    spot = jnp.arange(16, dtype=jnp.int32)
    step = jnp.array(OFFS, jnp.int32)
    inner, outer = step[spot % 4], step[spot // 4]

    def owners(core):
        along_y = jnp.where(core == 0, inner, outer)
        along_z = jnp.where(core == 0, outer, inner)
        return ((z + along_z) % 4) * 8 + ((y + along_y) % 4) * 2 + core

    owner = jnp.concatenate([owners(c), owners(1 - c)])
    tab = pairing.reshape(32, 2)[owner].reshape(64)
    own_pos = lax.dynamic_slice_in_dim(pairing, 2 * ctx, 2)
    rows = (own_pos[:, None] * BLK + jnp.arange(BLK, dtype=jnp.int32)[None, :]).reshape(ROWS)
    frequency = BASE ** (-(jnp.arange(HD // 2, dtype=F32) * 2.0 / HD))
    angle = rows.astype(F32)[:, None] * frequency[None, :]
    cos1, sin1 = jnp.cos(angle), jnp.sin(angle)
    cos = jnp.concatenate([cos1] * 4, 1)
    sin = jnp.concatenate([-sin1, sin1] * 2, 1)
    spots = [x, c, jnp.where(c == 0, y, z), jnp.where(c == 0, z, y)]
    place = jnp.stack(spots).astype(jnp.int32)

    act = (ROWS, D)
    stream0 = tokens[0]
    normed0, q0, kv0, wqkv0, gains = call(
        first_kernel,
        [(act, BF), (act, BF), ((ROWS, 384), BF), ((D, 960), BF), ((8, D), F32)],
        [place, stream0, *first_pieces, cos, sin],
        smem=1,
        scratch=[pltpu.VMEM((D, 1024), BF)],
        us=3.0,
        name="project_first",
    )

    def attend(q, kv):
        return call(
            attend_kernel,
            [
                ((SEQ, KW), BF),
                ((SEQ, KW), BF),
                ((2, KW, D), F32),
                ((2, 8, D), F32),
                (act, BF),
            ],
            [tab, own_pos, q, *kv],
            smem=2,
            scratch=[pltpu.VMEM((D, KW), BF), pltpu.VMEM((KW, D), F32), pltpu.VMEM((8, D), F32)],
            us=12.0,
            name="attend",
        )

    ffn0 = gather_ffn(after(halves(0), *first_pieces[1:3]))
    kv0, first0 = gather_plane(kv0)
    ffn1 = gather_ffn(after(halves(1), first0))
    ffn0 = [ffn0, send(after(ffn0, *kv0[:4]), other_core)]
    kp0, vp0, ot0, lse0, att0 = attend(q0, kv0)
    rest = rest + swap([after(r, att0) for r in rest])
    middle0, n20, stream1, normed1, q1, kv1, wo0, wqkv1, wo1 = call(
        middle_first_kernel,
        [
            (act, F32),
            (act, BF),
            (act, F32),
            (act, BF),
            (act, BF),
            ((ROWS, 384), BF),
            ((D, D), BF),
            ((D, 960), BF),
            ((D, D), BF),
        ],
        [place, stream0, att0, gains, *ffn0, *rest, cos, sin],
        smem=1,
        us=8.0,
        name="middle_first",
    )
    kv1, _ = gather_plane(kv1)
    ffn1 = [ffn1, send(after(ffn1, *kv1[:4]), other_core)]
    kp1, vp1, ot1, lse1, att1 = attend(q1, kv1)
    middle1, n21, out = call(
        middle_last_kernel,
        [(act, F32), (act, BF), ((D, ROWS), F32)],
        [stream1, att1, wo1, gains, *ffn1],
        us=6.0,
        name="middle_last",
    )

    def ffn_back(layer, grad, middle, n2, att, wo, ffn, waits=()):
        g_oth, part = call(
            ffn_back_other_kernel,
            [((4, D, D), BF), (act, F32)],
            [grad, n2, ffn[1]],
            us=5.0,
            name="ffn_back_other",
        )
        g_oth = send(g_oth, other_core)
        g_own, mid_grad, d_out, *small = call(
            functools.partial(ffn_back_own_kernel, 2 * layer),
            [((4, D, D), BF), (act, F32), (act, BF), ((D, D), BF), ((8, D), F32)],
            [grad, n2, ffn[0], after(part, *waits), middle, att, wo, gains],
            us=6.0,
            name="ffn_back_own",
        )
        half = total([g_own, g_oth]).astype(BF)
        return after(d_out, half), half, mid_grad, small

    def attend_back(q, d_out, kp, vp, ot, lse):
        return call(
            attend_back_kernel,
            [((2048, 384), BF), ((2048, 384), BF), (act, BF)],
            [tab, own_pos, q, d_out, kp, vp, ot, lse, cos, sin],
            smem=2,
            scratch=[
                pltpu.VMEM((D, KW), BF),
                pltpu.VMEM((D, KW), BF),
                pltpu.VMEM((SEQ, KW), F32),
                pltpu.VMEM((SEQ, KW), F32),
                pltpu.VMEM((KW, D), F32),
                pltpu.VMEM((ROWS, 640), F32),
            ],
            us=20.0,
            name="attend_back",
        )

    def project_back(layer, terms, dq_pre, normed, stream, wqkv, mid_grad, d_wo, d_gain_two):
        return call(
            functools.partial(project_back_kernel, 2 * layer),
            [((D, ROWS) if layer == 0 else act, F32), ((4, 224, D), BF), ((4, 224, D), BF)],
            [place, *terms, dq_pre, normed, stream, gains, wqkv, mid_grad, d_wo, d_gain_two, cos, sin],
            smem=1,
            scratch=[
                pltpu.VMEM((ROWS, 256), F32),
                pltpu.VMEM((2, D, D), BF),
                pltpu.VMEM((D, D), BF),
            ],
            us=5.0,
            name="project_back",
        )

    def share(half, order):
        return scatter_stage([half[j] for j in order], along_x)

    owners_x = [(x + k) % 4 for k in OFFS]

    d_out, half, mid_grad, small = ffn_back(1, cotangent[0], middle1, n21, att1, wo1, ffn1)
    g_ffn1 = share(half, owners_x)
    dkv_own, dkv_oth, dq_pre = attend_back(q1, d_out, kp1, vp1, ot1, lse1)
    terms = scatter_plane(dkv_own, after(dkv_oth, *g_ffn1[1:3]), g_ffn1[3:])
    grad1, a_own, a_oth = project_back(
        1, terms, dq_pre, normed1, stream1, wqkv1, mid_grad, *small
    )

    half_attn = add_cores(a_own, a_oth)
    g_attn1 = share(half_attn, range(4))
    d_out, half, mid_grad, small = ffn_back(
        0, grad1, middle0, n20, att0, wo0, ffn0, [half_attn]
    )
    g_ffn0 = share(half, owners_x)
    dkv_own, dkv_oth, dq_pre = attend_back(q0, after(d_out, *g_attn1), kp0, vp0, ot0, lse0)
    terms = scatter_plane(dkv_own, after(dkv_oth, *g_ffn0[1:3]), g_ffn0[3:])
    grad0, a_own, a_oth = project_back(
        0, terms, dq_pre, normed0, stream0, wqkv0, mid_grad, *small
    )
    g_attn0 = share(add_cores(a_own, a_oth), range(4))

    cut = call(
        pack_kernel,
        [((PACK // 4, D), BF)] * 4,
        [place, *g_ffn0, *g_ffn1, *g_attn0, *g_attn1],
        smem=1,
        scratch=[pltpu.VMEM((PACK, D), BF)],
        us=3.0,
        name="pack",
    )
    piece = total(scatter_stage(cut, plane_one)).astype(BF)
    piece = total(gather_stage(piece, plane_two)).astype(BF)
    mine = gather_stage(piece, plane_one)
    *grads, gain_sums = call(
        unpack_kernel,
        [
            ((2, 144, D), F32),
            ((2, 144, KW), F32),
            ((2, 144, KW), F32),
            ((2, 144, D), F32),
            ((2, D, 384), F32),
            ((2, D, 384), F32),
            ((2, D, 384), F32),
            ((16, D), F32),
        ],
        [place, *mine, *swap(mine)],
        smem=1,
        scratch=[pltpu.VMEM((PACK, D), BF), pltpu.VMEM((PACK, D), BF), pltpu.VMEM((384, D), F32)],
        us=6.0,
        name="unpack",
    )
    own_gains = lax.dynamic_slice_in_dim(gain_sums, 144 * x, 144, 1).reshape(2, 8, 144)
    grads[6] = jnp.swapaxes(grads[6], 1, 2)
    return (out.T[None], grad0.T[None], *grads, own_gains[:, 0], own_gains[:, 1])


def solution(mesh):
    rows = P("fsdp", "ctx", None)
    wide = P(None, "fsdp", None)
    deep = P(None, None, "fsdp")
    flat = P(None, "fsdp")
    return jax.shard_map(
        local,
        mesh=mesh,
        in_specs=(rows, P(), rows, wide, wide, wide, wide, deep, deep, wide, flat, flat),
        out_specs=(rows, rows, wide, wide, wide, wide, deep, deep, wide, flat, flat),
        check_vma=False,
    )
```

```python
import functools

import jax
import jax.numpy as jnp
from jax import lax
from jax.experimental import pallas as pl
from jax.experimental.pallas import tpu as pltpu
from jax.sharding import PartitionSpec as P

D = 576
HQ = 9
HK = 3
HD = 64
FF = 1536
BLK = 64
ROWS = 128
SEQ = 4096
KW = 192
CH_FORWARD = 1024
CH_BACK = 512
EPS = 1e-05
BASE = 100000.0
NEG = -1e30
F32 = jnp.float32
BF = jnp.bfloat16
AXES = ("ctx", "fsdp")
OFFS = (0, -1, 1, 2)
PACK = 2 * D + 2 * 224


def nn(a, b):
    return lax.dot_general(a, b, (((1,), (0,)), ((), ())), preferred_element_type=F32)


def nt(a, b):
    return lax.dot_general(a, b, (((1,), (1,)), ((), ())), preferred_element_type=F32)


def tn(a, b):
    return lax.dot_general(a, b, (((0,), (0,)), ((), ())), preferred_element_type=F32)


def pairs(move):
    found = []
    for z in range(4):
        for y in range(4):
            for c in range(2):
                for x in range(4):
                    a, b, e, f = move(z, y, c, x)
                    found.append(
                        (
                            ((z * 4 + y) * 2 + c) * 4 + x,
                            (((a % 4) * 4 + b % 4) * 2 + e) * 4 + f % 4,
                        )
                    )
    return found


def send(value, move):
    return lax.ppermute(value, AXES, pairs(move))


def plane(stage, k):
    def move(z, y, c, x):
        if (c + stage) % 2 == 0:
            return z, y + k, c, x
        return z + k, y, c, x

    return move


def along_x(k):
    return lambda z, y, c, x: (z, y, c, x + k)


def other_core(z, y, c, x):
    return z, y, 1 - c, x


def gather_stage(value, shift):
    return [value, send(value, shift(1)), send(value, shift(-1)), send(value, shift(2))]


def scatter_stage(parts, shift):
    return [
        parts[0],
        send(parts[1], shift(-1)),
        send(parts[2], shift(1)),
        send(parts[3], shift(2)),
    ]


def after(value, *others):
    return lax.optimization_barrier((value, *others))[0]


def total(parts):
    return sum(p.astype(F32) for p in parts)


def plane_one(k):
    return plane(0, k)


def plane_two(k):
    return plane(1, k)


def swap(values):
    return [send(v, other_core) for v in values]


def gather_plane(value):
    first = jnp.concatenate(gather_stage(value, plane_one), 0)
    own = gather_stage(first, plane_two)
    return own + swap(own), first


def scatter_plane(own, other):
    both = total([own, send(other, other_core)]).astype(BF)
    parts = both.reshape((4, 512) + own.shape[1:])
    one = total(scatter_stage([parts[j] for j in range(4)], plane_two)).astype(BF)
    one = one.reshape((4, 128) + own.shape[1:])
    return scatter_stage([one[j] for j in range(4)], plane_one)


def add_cores(own, other):
    return total([own, send(other, other_core)]).astype(BF)


def call(body, outs, args, smem=0, scratch=(), us=5.0, name=None):
    specs = [pl.BlockSpec(memory_space=pltpu.SMEM)] * smem
    specs += [pl.BlockSpec(memory_space=pltpu.VMEM)] * (len(args) - smem)
    return pl.pallas_call(
        body,
        out_shape=[jax.ShapeDtypeStruct(s, d) for s, d in outs],
        in_specs=specs,
        out_specs=[pl.BlockSpec(memory_space=pltpu.VMEM)] * len(outs),
        scratch_shapes=list(scratch),
        compiler_params=pltpu.CompilerParams(vmem_limit_bytes=58 * 1024 * 1024),
        cost_estimate=pl.CostEstimate(
            flops=int(us * 1.1e9), bytes_accessed=1000000, transcendentals=0
        ),
        name=name,
    )(*args)


def spin(v, cos, sin, back=False):
    lane = lax.broadcasted_iota(jnp.int32, (v.shape[0], 128), 1)
    low = (lane % 64) < 32
    pieces = []
    for j in range(v.shape[1] // 128):
        part = v[:, 128 * j : 128 * j + 128]
        swapped = jnp.where(low, pltpu.roll(part, 96, 1), pltpu.roll(part, 32, 1))
        if back:
            pieces.append(part * cos - swapped * sin)
        else:
            pieces.append(part * cos + swapped * sin)
    return jnp.concatenate(pieces, 1)


def rms(x):
    return lax.rsqrt(jnp.mean(x * x, axis=-1, keepdims=True) + EPS)


def norm_back(x, gain, grad):
    r = rms(x)
    inner = jnp.mean(grad * gain * x, axis=-1, keepdims=True)
    d_x = r * gain * grad - x * (r * r * r * inner)
    d_gain = jnp.sum(grad * x * r, axis=0, keepdims=True)
    return d_x, d_gain


def project(normed, weight, cos, sin, q_ref, kv_ref):
    mixed = nn(normed, weight)
    turned = spin(mixed[:, :768], cos, sin)
    q_ref[...] = (turned[:, :D].astype(BF).astype(F32) * (HD**-0.5)).astype(BF)
    kv_ref[:, :KW] = turned[:, D:768].astype(BF)
    kv_ref[:, KW:] = mixed[:, 768:960].astype(BF)


def first_kernel(x_ref, tok, p0, p1, p2, p3, cos, sin, normed, q, kv, w, gains, tmp):
    for j, piece in enumerate((p0, p1, p2, p3)):
        owner = lax.rem(x_ref[0] + (OFFS[j] + 4), 4)
        tmp[pl.ds(pl.multiple_of(owner * 144, 16), 144), :] = piece[...]
    w[...] = tmp[:, :960]
    g = tmp[:, 896:1024].astype(F32).T
    gains[...] = g[64:72, :]
    x = tok[...].astype(F32)
    n = (x * rms(x) * g[64:65, :]).astype(BF)
    normed[...] = n
    project(n, w[...], cos[...], sin[...], q, kv)


def spread(src, dst, block):
    dst[...] = jnp.zeros(dst.shape, BF)
    for h in range(HQ):
        g = h // 3
        dst[HD * h : HD * h + HD, HD * g : HD * g + HD] = src[
            BLK * block : BLK * block + BLK, HD * h : HD * h + HD
        ]


def allowed(chunk, position, size):
    key = lax.broadcasted_iota(jnp.int32, (size, D), 0) + chunk * size
    query = (lax.broadcasted_iota(jnp.int32, (size, D), 1) % BLK) + position * BLK
    return key <= query


def attend_kernel(tab, own_pos, q, *rest):
    kv, (kp, vp, ot, lse, att, qbd, acc, stat) = rest[:8], rest[8:]

    def place(s, carry):
        for j, ref in enumerate(kv):
            at = pl.ds(pl.multiple_of(tab[8 * j + s] * BLK, BLK), BLK)
            rows = ref[pl.ds(pl.multiple_of(s * BLK, BLK), BLK), :]
            kp[at, :] = rows[:, :KW]
            vp[at, :] = rows[:, KW:]
        return carry

    lax.fori_loop(0, 8, place, 0)
    for block in range(2):
        position = own_pos[block]
        spread(q, qbd, block)
        stat[0:1, :] = jnp.full((1, D), NEG, F32)
        stat[1:2, :] = jnp.zeros((1, D), F32)
        acc[...] = jnp.zeros((KW, D), F32)

        def step(i, masked):
            at = pl.ds(pl.multiple_of(i * CH_FORWARD, CH_FORWARD), CH_FORWARD)
            s = nt(kp[at, :], qbd[...])
            if masked:
                s = jnp.where(allowed(i, position, CH_FORWARD), s, NEG)
            old = stat[0:1, :]
            new = jnp.maximum(old, jnp.max(s, axis=0, keepdims=True))
            p = jnp.exp(s - new)
            fade = jnp.exp(old - new)
            stat[0:1, :] = new
            stat[1:2, :] = stat[1:2, :] * fade + jnp.sum(p, axis=0, keepdims=True)
            acc[...] = acc[...] * fade + tn(vp[at, :], p.astype(BF))

        def loop(i, carry):
            step(i, False)
            return carry

        last = position // (CH_FORWARD // BLK)
        lax.fori_loop(0, last, loop, 0)
        step(last, True)
        result = acc[...] / stat[1:2, :]
        ot[block] = result
        lse[block] = jnp.broadcast_to(stat[0:1, :] + jnp.log(stat[1:2, :]), (8, D))
        turned = result.T
        for h in range(HQ):
            g = h // 3
            att[BLK * block : BLK * block + BLK, HD * h : HD * h + HD] = turned[
                HD * h : HD * h + HD, HD * g : HD * g + HD
            ].astype(BF)


def ffn_forward(n2, pieces):
    out = None
    for ref in pieces:
        for k in range(4):
            gate = nt(n2, ref[k, 0:KW, :])
            up = nt(n2, ref[k, KW : 2 * KW, :])
            hidden = (gate * jax.nn.sigmoid(gate) * up).astype(BF)
            term = nn(hidden, ref[k, 2 * KW : 3 * KW, :])
            out = term if out is None else out + term
    return out


def middle_first_kernel(
    place, stream, att, gains, w, v, r0, r1, r2, r3, s0, s1, s2, s3, cos, sin,
    middle_ref, n2_ref, out, normed, q, kv, wo0, wqkv1, wo1,
):
    x, c = place[0], place[1]

    def sort(outs, projections):
        for j in range(4):
            owner = lax.rem(x + (OFFS[j] + 4), 4)
            at = pl.ds(pl.multiple_of(owner * 144, 16), 144)
            wo0[at, :] = outs[j][:, :D]
            wo1[at, :] = outs[j][:, D:]
            wqkv1[at, :] = projections[j][:, :960]

    @pl.when(c == 0)
    def _():
        sort((r0, r1, r2, r3), (s0, s1, s2, s3))

    @pl.when(c == 1)
    def _():
        sort((s0, s1, s2, s3), (r0, r1, r2, r3))

    middle = stream[...].astype(F32) + nn(att[...], wo0[...])
    middle_ref[...] = middle
    n2 = (middle * rms(middle) * gains[1:2, :]).astype(BF)
    n2_ref[...] = n2
    result = middle + ffn_forward(n2, (w, v))
    out[...] = result
    n = (result * rms(result) * gains[2:3, :]).astype(BF)
    normed[...] = n
    project(n, wqkv1[...], cos[...], sin[...], q, kv)


def middle_last_kernel(stream, att, wo, gains, w, v, middle_ref, n2_ref, out):
    middle = stream[...] + nn(att[...], wo[...])
    middle_ref[...] = middle
    n2 = (middle * rms(middle) * gains[3:4, :]).astype(BF)
    n2_ref[...] = n2
    out[...] = (middle + ffn_forward(n2, (w, v))).T


def ffn_grads(branch, n2, weights, dst):
    n2_grad = None
    for k in range(4):
        p = weights.at[k]
        gate = nt(n2, p[0:KW, :])
        up = nt(n2, p[KW : 2 * KW, :])
        s = jax.nn.sigmoid(gate)
        hidden = (gate * s * up).astype(BF)
        hidden_grad = nt(branch, p[2 * KW : 3 * KW, :])
        gate_grad = (hidden_grad * up * s * (1.0 + gate * (1.0 - s))).astype(BF)
        up_grad = (hidden_grad * gate * s).astype(BF)
        dst[k, 0:KW, :] = tn(gate_grad, n2).astype(BF)
        dst[k, KW : 2 * KW, :] = tn(up_grad, n2).astype(BF)
        dst[k, 2 * KW : 3 * KW, :] = tn(hidden, branch).astype(BF)
        term = nn(gate_grad, p[0:KW, :]) + nn(up_grad, p[KW : 2 * KW, :])
        n2_grad = term if n2_grad is None else n2_grad + term
    return n2_grad


def ffn_back_other_kernel(grad, n2, v, g_oth, part):
    part[...] = ffn_grads(grad[...].astype(BF), n2[...], v, g_oth)


def ffn_back_own_kernel(
    gain_row, grad, n2, w, half_grad, middle, att, wo, gains, g_own, mid_grad, d_out, d_wo, d_gain
):
    g = grad[...]
    n2_grad = half_grad[...] + ffn_grads(g.astype(BF), n2[...], w, g_own)
    part, gain_grad = norm_back(middle[...], gains[gain_row + 1 : gain_row + 2, :], n2_grad)
    m_grad = g + part
    mid_grad[...] = m_grad
    d_gain[...] = jnp.broadcast_to(gain_grad, (8, D))
    ab = m_grad.astype(BF)
    d_wo[...] = tn(att[...], ab).astype(BF)
    d_out[...] = nt(ab, wo[...]).astype(BF)


def attend_back_kernel(
    tab, own_pos, q, d_out, kp, vp, ot, lse, cos, sin, dkv_own, dkv_oth, dq_pre,
    qbd, dbd, dk, dv, dqt, flat,
):
    dk[...] = jnp.zeros(dk.shape, F32)
    dv[...] = jnp.zeros(dv.shape, F32)
    flat[:, D:] = jnp.zeros((ROWS, 64), F32)
    for block in range(2):
        position = own_pos[block]
        spread(q, qbd, block)
        spread(d_out, dbd, block)
        delta = jnp.sum(ot[block] * dbd[...].astype(F32).T, axis=0, keepdims=True)
        log_total = lse[block][0:1, :]
        dqt[...] = jnp.zeros((KW, D), F32)

        def step(i, masked):
            at = pl.ds(pl.multiple_of(i * CH_BACK, CH_BACK), CH_BACK)
            p = jnp.exp(nt(kp[at, :], qbd[...]) - log_total)
            if masked:
                p = jnp.where(allowed(i, position, CH_BACK), p, 0.0)
            p_grad = nt(vp[at, :], dbd[...])
            s_grad = (p * (p_grad - delta)).astype(BF)
            dv[at, :] += nn(p.astype(BF), dbd[...])
            dk[at, :] += nn(s_grad, qbd[...])
            dqt[...] += tn(kp[at, :], s_grad)

        def loop(i, carry):
            step(i, False)
            return carry

        last = position // (CH_BACK // BLK)
        lax.fori_loop(0, last, loop, 0)
        step(last, True)
        turned = (dqt[...] * (HD**-0.5)).T
        for h in range(HQ):
            g = h // 3
            flat[BLK * block : BLK * block + BLK, HD * h : HD * h + HD] = turned[
                HD * h : HD * h + HD, HD * g : HD * g + HD
            ]
    dq_pre[...] = spin(flat[...], cos[...], sin[...], True)[:, :D].astype(BF)

    def place(s, carry):
        for base, ref in ((0, dkv_own), (32, dkv_oth)):
            at = pl.ds(pl.multiple_of(tab[base + s] * BLK, BLK), BLK)
            to = pl.ds(pl.multiple_of(s * BLK, BLK), BLK)
            ref[to, :] = jnp.concatenate([dk[at, :].astype(BF), dv[at, :].astype(BF)], 1)
        return carry

    lax.fori_loop(0, 32, place, 0)


def project_back_kernel(
    gain_row, place_ref, t0, t1, t2, t3, dq_pre, normed, stream, gains, wqkv, mid_grad,
    d_wo, d_gain_two, cos, sin, grad, g_own, g_oth, kbuf, full, side,
):
    x, c = place_ref[0], place_ref[1]
    dkv = t0[...].astype(F32) + t1[...].astype(F32) + t2[...].astype(F32) + t3[...].astype(F32)
    kbuf[:, :KW] = dkv[:, :KW]
    kbuf[:, KW:] = jnp.zeros((ROWS, 64), F32)
    dk_pre = spin(kbuf[...], cos[...], sin[...], True)[:, :KW].astype(BF)
    dqk = jnp.concatenate([dq_pre[...], dk_pre], 1)
    dv_pre = dkv[:, KW:].astype(BF)
    n = normed[...]
    full[0] = tn(n, dq_pre[...]).astype(BF)
    full[1] = d_wo[...]
    side[:, : 2 * KW] = tn(n, jnp.concatenate([dk_pre, dv_pre], 1)).astype(BF)
    side[:, 2 * KW :] = jnp.zeros((D, KW), BF)
    n_grad = nt(jnp.concatenate([dqk, dv_pre], 1), wqkv[...])
    part, gain_grad = norm_back(stream[...].astype(F32), gains[gain_row : gain_row + 1, :], n_grad)
    total_grad = mid_grad[...] + part
    grad[...] = total_grad.T if grad.shape[0] == D else total_grad
    row = lax.broadcasted_iota(jnp.int32, (16, D), 0)
    both_gains = jnp.where(row == 0, gain_grad, d_gain_two[0:1, :]).astype(BF)

    def write(low, high):
        for j in range(4):
            start = pl.multiple_of(lax.rem(x + (OFFS[j] + 4), 4) * 144, 16)
            low[j, :144, :] = full[0, pl.ds(start, 144), :]
            high[j, :144, :] = full[1, pl.ds(start, 144), :]
            low[j, 144:, :] = side[pl.ds(start, 80), :]
            high[j, 144:208, :] = side[pl.ds(start + 80, 64), :]
            high[j, 208:, :] = both_gains

    @pl.when(c == 0)
    def _():
        write(g_own, g_oth)

    @pl.when(c == 1)
    def _():
        write(g_oth, g_own)


def pack_kernel(place, *refs):
    ffn0, ffn1, attn1, attn0, outs, tmp = *refs[:3], refs[3:7], refs[7:11], refs[11]
    tmp[:D, :] = ffn0[...]
    tmp[D : 2 * D, :] = ffn1[...]
    tmp[2 * D : 2 * D + 224, :] = sum(r[...].astype(F32) for r in attn0).astype(BF)
    tmp[2 * D + 224 :, :] = attn1[...]
    for j in range(4):
        start = lax.rem(place[2] + (OFFS[j] + 4), 4) * (PACK // 4)
        outs[j][...] = tmp[pl.ds(pl.multiple_of(start, 16), PACK // 4), :]


def unpack_kernel(
    place, m0, m1, m2, m3, t0, t1, t2, t3,
    dq, dk, dv, do, dg, du, dd, gains, mine, theirs, turn,
):
    c = place[1]
    for j in range(4):
        start = lax.rem(place[2] + (OFFS[j] + 4), 4) * (PACK // 4)
        mine[pl.ds(pl.multiple_of(start, 16), PACK // 4), :] = (m0, m1, m2, m3)[j][...]
        start = lax.rem(place[3] + (OFFS[j] + 4), 4) * (PACK // 4)
        theirs[pl.ds(pl.multiple_of(start, 16), PACK // 4), :] = (t0, t1, t2, t3)[j][...]
    for layer in range(2):
        a, b = mine.at[D * layer : D * layer + D], theirs.at[D * layer : D * layer + D]
        at_a = pl.ds(pl.multiple_of(c * KW, 64), KW)
        at_b = pl.ds(pl.multiple_of((1 - c) * KW, 64), KW)
        for k, ref in enumerate((dg, du, dd)):
            turn[at_a, :] = a[KW * k : KW * k + KW, :].astype(F32)
            turn[at_b, :] = b[KW * k : KW * k + KW, :].astype(F32)
            ref[layer] = turn[...].T

    def write(low, high):
        for layer in range(2):
            at = 2 * D + 224 * layer
            dq[layer] = low[at : at + 144, :].astype(F32)
            do[layer] = high[at : at + 144, :].astype(F32)
            for ref, lanes in ((dk, slice(0, KW)), (dv, slice(KW, 2 * KW))):
                ref[layer, :80, :] = low[at + 144 : at + 224, lanes].astype(F32)
                ref[layer, 80:, :] = high[at + 144 : at + 208, lanes].astype(F32)
            gains[8 * layer : 8 * layer + 8, :] = high[at + 208 : at + 224, :].astype(F32)[:8, :]

    @pl.when(c == 0)
    def _():
        write(mine, theirs)

    @pl.when(c == 1)
    def _():
        write(theirs, mine)


def local(tokens, pairing, cotangent, w_query, w_key, w_value, w_out, w_gate, w_up, w_down, attn_gain, ffn_gain):
    ctx = lax.axis_index("ctx")
    x = lax.axis_index("fsdp")
    z, y, c = ctx // 8, (ctx // 2) % 4, ctx % 2

    gains_in = jnp.stack([attn_gain[0], ffn_gain[0], attn_gain[1], ffn_gain[1]], 1)
    bundle = jnp.concatenate(
        [w_query[0], w_key[0], w_value[0], gains_in, jnp.zeros((144, 60), BF)], 1
    )
    w_gate, w_up, w_down, w_out = after((w_gate, w_up, w_down, w_out), bundle)
    first_pieces = gather_stage(bundle, along_x)
    outs = jnp.concatenate([w_out[0], w_out[1]], 1)
    later = jnp.concatenate([w_query[1], w_key[1], w_value[1], jnp.zeros((144, KW), BF)], 1)
    rest = gather_stage(jnp.where(c == 0, outs, later), along_x)

    def halves(layer):
        parts = [
            lax.dynamic_slice_in_dim(m, KW * c, KW, 0)
            for m in (w_gate[layer].T, w_up[layer].T, w_down[layer])
        ]
        return jnp.concatenate(parts, 0)

    def gather_ffn(mine):
        return lax.all_gather(mine, "fsdp", axis=0)

    spot = jnp.arange(16, dtype=jnp.int32)
    step = jnp.array(OFFS, jnp.int32)
    inner, outer = step[spot % 4], step[spot // 4]

    def owners(core):
        along_y = jnp.where(core == 0, inner, outer)
        along_z = jnp.where(core == 0, outer, inner)
        return ((z + along_z) % 4) * 8 + ((y + along_y) % 4) * 2 + core

    owner = jnp.concatenate([owners(c), owners(1 - c)])
    tab = pairing.reshape(32, 2)[owner].reshape(64)
    own_pos = lax.dynamic_slice_in_dim(pairing, 2 * ctx, 2)
    rows = (own_pos[:, None] * BLK + jnp.arange(BLK, dtype=jnp.int32)[None, :]).reshape(ROWS)
    frequency = BASE ** (-(jnp.arange(HD // 2, dtype=F32) * 2.0 / HD))
    angle = rows.astype(F32)[:, None] * frequency[None, :]
    cos1, sin1 = jnp.cos(angle), jnp.sin(angle)
    cos = jnp.concatenate([cos1] * 4, 1)
    sin = jnp.concatenate([-sin1, sin1] * 2, 1)
    spots = [x, c, jnp.where(c == 0, y, z), jnp.where(c == 0, z, y)]
    place = jnp.stack(spots).astype(jnp.int32)

    act = (ROWS, D)
    stream0 = tokens[0]
    normed0, q0, kv0, wqkv0, gains = call(
        first_kernel,
        [(act, BF), (act, BF), ((ROWS, 384), BF), ((D, 960), BF), ((8, D), F32)],
        [place, stream0, *first_pieces, cos, sin],
        smem=1,
        scratch=[pltpu.VMEM((D, 1024), BF)],
        us=3.0,
        name="project_first",
    )

    def attend(q, kv):
        return call(
            attend_kernel,
            [
                ((SEQ, KW), BF),
                ((SEQ, KW), BF),
                ((2, KW, D), F32),
                ((2, 8, D), F32),
                (act, BF),
            ],
            [tab, own_pos, q, *kv],
            smem=2,
            scratch=[pltpu.VMEM((D, KW), BF), pltpu.VMEM((KW, D), F32), pltpu.VMEM((8, D), F32)],
            us=12.0,
            name="attend",
        )

    ffn0 = gather_ffn(halves(0))
    kv0, first0 = gather_plane(kv0)
    ffn1 = gather_ffn(after(halves(1), first0))
    ffn0 = [ffn0, send(after(ffn0, *kv0[:4]), other_core)]
    kp0, vp0, ot0, lse0, att0 = attend(q0, kv0)
    rest = rest + swap([after(r, att0) for r in rest])
    middle0, n20, stream1, normed1, q1, kv1, wo0, wqkv1, wo1 = call(
        middle_first_kernel,
        [
            (act, F32),
            (act, BF),
            (act, F32),
            (act, BF),
            (act, BF),
            ((ROWS, 384), BF),
            ((D, D), BF),
            ((D, 960), BF),
            ((D, D), BF),
        ],
        [place, stream0, att0, gains, *ffn0, *rest, cos, sin],
        smem=1,
        us=8.0,
        name="middle_first",
    )
    kv1, _ = gather_plane(kv1)
    ffn1 = [ffn1, send(after(ffn1, *kv1[:4]), other_core)]
    kp1, vp1, ot1, lse1, att1 = attend(q1, kv1)
    middle1, n21, out = call(
        middle_last_kernel,
        [(act, F32), (act, BF), ((D, ROWS), F32)],
        [stream1, att1, wo1, gains, *ffn1],
        us=6.0,
        name="middle_last",
    )

    def ffn_back(layer, grad, middle, n2, att, wo, ffn, waits=()):
        g_oth, part = call(
            ffn_back_other_kernel,
            [((4, D, D), BF), (act, F32)],
            [grad, n2, ffn[1]],
            us=5.0,
            name="ffn_back_other",
        )
        g_oth = send(g_oth, other_core)
        g_own, mid_grad, d_out, *small = call(
            functools.partial(ffn_back_own_kernel, 2 * layer),
            [((4, D, D), BF), (act, F32), (act, BF), ((D, D), BF), ((8, D), F32)],
            [grad, n2, ffn[0], after(part, *waits), middle, att, wo, gains],
            us=6.0,
            name="ffn_back_own",
        )
        half = total([g_own, g_oth]).astype(BF)
        return after(d_out, half), half, mid_grad, small

    def attend_back(q, d_out, kp, vp, ot, lse):
        return call(
            attend_back_kernel,
            [((2048, 384), BF), ((2048, 384), BF), (act, BF)],
            [tab, own_pos, q, d_out, kp, vp, ot, lse, cos, sin],
            smem=2,
            scratch=[
                pltpu.VMEM((D, KW), BF),
                pltpu.VMEM((D, KW), BF),
                pltpu.VMEM((SEQ, KW), F32),
                pltpu.VMEM((SEQ, KW), F32),
                pltpu.VMEM((KW, D), F32),
                pltpu.VMEM((ROWS, 640), F32),
            ],
            us=20.0,
            name="attend_back",
        )

    def project_back(layer, terms, dq_pre, normed, stream, wqkv, mid_grad, d_wo, d_gain_two):
        return call(
            functools.partial(project_back_kernel, 2 * layer),
            [((D, ROWS) if layer == 0 else act, F32), ((4, 224, D), BF), ((4, 224, D), BF)],
            [place, *terms, dq_pre, normed, stream, gains, wqkv, mid_grad, d_wo, d_gain_two, cos, sin],
            smem=1,
            scratch=[
                pltpu.VMEM((ROWS, 256), F32),
                pltpu.VMEM((2, D, D), BF),
                pltpu.VMEM((D, D), BF),
            ],
            us=5.0,
            name="project_back",
        )

    def share(half, order):
        return scatter_stage([half[j] for j in order], along_x)

    owners_x = [(x + k) % 4 for k in OFFS]

    d_out, half, mid_grad, small = ffn_back(1, cotangent[0], middle1, n21, att1, wo1, ffn1)
    g_ffn1 = share(half, owners_x)
    dkv_own, dkv_oth, dq_pre = attend_back(q1, d_out, kp1, vp1, ot1, lse1)
    terms = scatter_plane(dkv_own, after(dkv_oth, *g_ffn1[1:3]))
    grad1, a_own, a_oth = project_back(
        1, terms, dq_pre, normed1, stream1, wqkv1, mid_grad, *small
    )

    half_attn = add_cores(a_own, a_oth)
    g_attn1 = share(half_attn, range(4))
    d_out, half, mid_grad, small = ffn_back(
        0, grad1, middle0, n20, att0, wo0, ffn0, [half_attn, g_ffn1[3]]
    )
    g_ffn0 = share(half, owners_x)
    dkv_own, dkv_oth, dq_pre = attend_back(q0, after(d_out, *g_attn1), kp0, vp0, ot0, lse0)
    terms = scatter_plane(dkv_own, after(dkv_oth, *g_ffn0[1:3]))
    grad0, a_own, a_oth = project_back(
        0, terms, dq_pre, normed0, stream0, wqkv0, mid_grad, *small
    )
    g_attn0 = share(after(add_cores(a_own, a_oth), g_ffn0[3]), range(4))

    cut = call(
        pack_kernel,
        [((PACK // 4, D), BF)] * 4,
        [place, *(total(g).astype(BF) for g in (g_ffn0, g_ffn1, g_attn1)), *g_attn0],
        smem=1,
        scratch=[pltpu.VMEM((PACK, D), BF)],
        us=3.0,
        name="pack",
    )
    piece = total(scatter_stage(cut, plane_one)).astype(BF)
    piece = total(gather_stage(piece, plane_two)).astype(BF)
    mine = gather_stage(piece, plane_one)
    *grads, gain_sums = call(
        unpack_kernel,
        [
            ((2, 144, D), F32),
            ((2, 144, KW), F32),
            ((2, 144, KW), F32),
            ((2, 144, D), F32),
            ((2, D, 384), F32),
            ((2, D, 384), F32),
            ((2, D, 384), F32),
            ((16, D), F32),
        ],
        [place, *mine, *swap(mine)],
        smem=1,
        scratch=[pltpu.VMEM((PACK, D), BF), pltpu.VMEM((PACK, D), BF), pltpu.VMEM((384, D), F32)],
        us=6.0,
        name="unpack",
    )
    own_gains = lax.dynamic_slice_in_dim(gain_sums, 144 * x, 144, 1).reshape(2, 8, 144)
    grads[6] = jnp.swapaxes(grads[6], 1, 2)
    return (out.T[None], grad0.T[None], *grads, own_gains[:, 0], own_gains[:, 1])


def solution(mesh):
    rows = P("fsdp", "ctx", None)
    wide = P(None, "fsdp", None)
    deep = P(None, None, "fsdp")
    flat = P(None, "fsdp")
    return jax.shard_map(
        local,
        mesh=mesh,
        in_specs=(rows, P(), rows, wide, wide, wide, wide, deep, deep, wide, flat, flat),
        out_specs=(rows, rows, wide, wide, wide, wide, deep, deep, wide, flat, flat),
        check_vma=False,
    )
```

```python
import functools

import jax
import jax.numpy as jnp
from jax import lax
from jax.experimental import pallas as pl
from jax.experimental.pallas import tpu as pltpu
from jax.sharding import PartitionSpec as P

D = 576
HQ = 9
HK = 3
HD = 64
FF = 1536
BLK = 64
ROWS = 128
SEQ = 4096
KW = 192
CH_FORWARD = 512
CH_BACK = 512
EPS = 1e-05
BASE = 100000.0
NEG = -1e30
F32 = jnp.float32
BF = jnp.bfloat16
AXES = ("ctx", "fsdp")
OFFS = (0, -1, 1, 2)
PACK = 2 * D + 2 * 224


def nn(a, b):
    return lax.dot_general(a, b, (((1,), (0,)), ((), ())), preferred_element_type=F32)


def nt(a, b):
    return lax.dot_general(a, b, (((1,), (1,)), ((), ())), preferred_element_type=F32)


def tn(a, b):
    return lax.dot_general(a, b, (((0,), (0,)), ((), ())), preferred_element_type=F32)


def pairs(move):
    found = []
    for z in range(4):
        for y in range(4):
            for c in range(2):
                for x in range(4):
                    a, b, e, f = move(z, y, c, x)
                    found.append(
                        (
                            ((z * 4 + y) * 2 + c) * 4 + x,
                            (((a % 4) * 4 + b % 4) * 2 + e) * 4 + f % 4,
                        )
                    )
    return found


def send(value, move):
    return lax.ppermute(value, AXES, pairs(move))


def plane(stage, k):
    def move(z, y, c, x):
        if (c + stage) % 2 == 0:
            return z, y + k, c, x
        return z + k, y, c, x

    return move


def along_x(k):
    return lambda z, y, c, x: (z, y, c, x + k)


def other_core(z, y, c, x):
    return z, y, 1 - c, x


def gather_stage(value, shift):
    return [value, send(value, shift(1)), send(value, shift(-1)), send(value, shift(2))]


def scatter_stage(parts, shift):
    return [
        parts[0],
        send(parts[1], shift(-1)),
        send(parts[2], shift(1)),
        send(parts[3], shift(2)),
    ]


def after(value, *others):
    return lax.optimization_barrier((value, *others))[0]


def total(parts):
    return sum(p.astype(F32) for p in parts)


def plane_one(k):
    return plane(0, k)


def plane_two(k):
    return plane(1, k)


def swap(values):
    return [send(v, other_core) for v in values]


def gather_plane(value):
    first = jnp.concatenate(gather_stage(value, plane_one), 0)
    own = gather_stage(first, plane_two)
    return own + swap(own), first


def scatter_plane(own, other):
    both = total([own, send(other, other_core)]).astype(BF)
    parts = both.reshape((4, 512) + own.shape[1:])
    one = total(scatter_stage([parts[j] for j in range(4)], plane_two)).astype(BF)
    one = one.reshape((4, 128) + own.shape[1:])
    return scatter_stage([one[j] for j in range(4)], plane_one)


def add_cores(own, other):
    return total([own, send(other, other_core)]).astype(BF)


def call(body, outs, args, smem=0, scratch=(), us=5.0, name=None):
    specs = [pl.BlockSpec(memory_space=pltpu.SMEM)] * smem
    specs += [pl.BlockSpec(memory_space=pltpu.VMEM)] * (len(args) - smem)
    return pl.pallas_call(
        body,
        out_shape=[jax.ShapeDtypeStruct(s, d) for s, d in outs],
        in_specs=specs,
        out_specs=[pl.BlockSpec(memory_space=pltpu.VMEM)] * len(outs),
        scratch_shapes=list(scratch),
        compiler_params=pltpu.CompilerParams(vmem_limit_bytes=58 * 1024 * 1024),
        cost_estimate=pl.CostEstimate(
            flops=int(us * 1.1e9), bytes_accessed=1000000, transcendentals=0
        ),
        name=name,
    )(*args)


def spin(v, cos, sin, back=False):
    lane = lax.broadcasted_iota(jnp.int32, (v.shape[0], 128), 1)
    low = (lane % 64) < 32
    pieces = []
    for j in range(v.shape[1] // 128):
        part = v[:, 128 * j : 128 * j + 128]
        swapped = jnp.where(low, pltpu.roll(part, 96, 1), pltpu.roll(part, 32, 1))
        if back:
            pieces.append(part * cos - swapped * sin)
        else:
            pieces.append(part * cos + swapped * sin)
    return jnp.concatenate(pieces, 1)


def rms(x):
    return lax.rsqrt(jnp.mean(x * x, axis=-1, keepdims=True) + EPS)


def norm_back(x, gain, grad):
    r = rms(x)
    inner = jnp.mean(grad * gain * x, axis=-1, keepdims=True)
    d_x = r * gain * grad - x * (r * r * r * inner)
    d_gain = jnp.sum(grad * x * r, axis=0, keepdims=True)
    return d_x, d_gain


def project(normed, weight, cos, sin, q_ref, kv_ref):
    mixed = nn(normed, weight)
    turned = spin(mixed[:, :768], cos, sin)
    q_ref[...] = (turned[:, :D].astype(BF).astype(F32) * (HD**-0.5)).astype(BF)
    kv_ref[:, :KW] = turned[:, D:768].astype(BF)
    kv_ref[:, KW:] = mixed[:, 768:960].astype(BF)


def first_kernel(x_ref, tok, p0, p1, p2, p3, cos, sin, normed, q, kv, w, gains, tmp):
    for j, piece in enumerate((p0, p1, p2, p3)):
        owner = lax.rem(x_ref[0] + (OFFS[j] + 4), 4)
        tmp[pl.ds(pl.multiple_of(owner * 144, 16), 144), :] = piece[...]
    w[...] = tmp[:, :960]
    g = tmp[:, 896:1024].astype(F32).T
    gains[...] = g[64:72, :]
    x = tok[...].astype(F32)
    n = (x * rms(x) * g[64:65, :]).astype(BF)
    normed[...] = n
    project(n, w[...], cos[...], sin[...], q, kv)


def spread(src, dst, block):
    dst[...] = jnp.zeros(dst.shape, BF)
    for h in range(HQ):
        g = h // 3
        dst[HD * h : HD * h + HD, HD * g : HD * g + HD] = src[
            BLK * block : BLK * block + BLK, HD * h : HD * h + HD
        ]


def allowed(chunk, position, size):
    key = lax.broadcasted_iota(jnp.int32, (size, D), 0) + chunk * size
    query = (lax.broadcasted_iota(jnp.int32, (size, D), 1) % BLK) + position * BLK
    return key <= query


def attend_kernel(tab, own_pos, q, *rest):
    kv, (kp, vp, ot, lse, att, qbd, acc, stat) = rest[:8], rest[8:]

    def place(s, carry):
        for j, ref in enumerate(kv):
            at = pl.ds(pl.multiple_of(tab[8 * j + s] * BLK, BLK), BLK)
            rows = ref[pl.ds(pl.multiple_of(s * BLK, BLK), BLK), :]
            kp[at, :] = rows[:, :KW]
            vp[at, :] = rows[:, KW:]
        return carry

    lax.fori_loop(0, 8, place, 0)
    for block in range(2):
        position = own_pos[block]
        spread(q, qbd, block)
        stat[0:1, :] = jnp.full((1, D), NEG, F32)
        stat[1:2, :] = jnp.zeros((1, D), F32)
        acc[...] = jnp.zeros((KW, D), F32)

        def step(i, masked):
            at = pl.ds(pl.multiple_of(i * CH_FORWARD, CH_FORWARD), CH_FORWARD)
            s = nt(kp[at, :], qbd[...])
            if masked:
                s = jnp.where(allowed(i, position, CH_FORWARD), s, NEG)
            old = stat[0:1, :]
            new = jnp.maximum(old, jnp.max(s, axis=0, keepdims=True))
            p = jnp.exp(s - new)
            fade = jnp.exp(old - new)
            stat[0:1, :] = new
            stat[1:2, :] = stat[1:2, :] * fade + jnp.sum(p, axis=0, keepdims=True)
            acc[...] = acc[...] * fade + tn(vp[at, :], p.astype(BF))

        def loop(i, carry):
            step(i, False)
            return carry

        last = position // (CH_FORWARD // BLK)
        lax.fori_loop(0, last, loop, 0)
        step(last, True)
        result = acc[...] / stat[1:2, :]
        ot[block] = result
        lse[block] = jnp.broadcast_to(stat[0:1, :] + jnp.log(stat[1:2, :]), (8, D))
        turned = result.T
        for h in range(HQ):
            g = h // 3
            att[BLK * block : BLK * block + BLK, HD * h : HD * h + HD] = turned[
                HD * h : HD * h + HD, HD * g : HD * g + HD
            ].astype(BF)


def ffn_forward(n2, pieces):
    out = None
    for ref in pieces:
        for k in range(4):
            gate = nt(n2, ref[k, 0:KW, :])
            up = nt(n2, ref[k, KW : 2 * KW, :])
            hidden = (gate * jax.nn.sigmoid(gate) * up).astype(BF)
            term = nn(hidden, ref[k, 2 * KW : 3 * KW, :])
            out = term if out is None else out + term
    return out


def middle_first_kernel(
    place, stream, att, gains, w, v, r0, r1, r2, r3, s0, s1, s2, s3, cos, sin,
    middle_ref, n2_ref, out, normed, q, kv, wo0, wqkv1, wo1,
):
    x, c = place[0], place[1]

    def sort(outs, projections):
        for j in range(4):
            owner = lax.rem(x + (OFFS[j] + 4), 4)
            at = pl.ds(pl.multiple_of(owner * 144, 16), 144)
            wo0[at, :] = outs[j][:, :D]
            wo1[at, :] = outs[j][:, D:]
            wqkv1[at, :] = projections[j][:, :960]

    @pl.when(c == 0)
    def _():
        sort((r0, r1, r2, r3), (s0, s1, s2, s3))

    @pl.when(c == 1)
    def _():
        sort((s0, s1, s2, s3), (r0, r1, r2, r3))

    middle = stream[...].astype(F32) + nn(att[...], wo0[...])
    middle_ref[...] = middle
    n2 = (middle * rms(middle) * gains[1:2, :]).astype(BF)
    n2_ref[...] = n2
    result = middle + ffn_forward(n2, (w, v))
    out[...] = result
    n = (result * rms(result) * gains[2:3, :]).astype(BF)
    normed[...] = n
    project(n, wqkv1[...], cos[...], sin[...], q, kv)


def middle_last_kernel(stream, att, wo, gains, w, v, middle_ref, n2_ref, out):
    middle = stream[...] + nn(att[...], wo[...])
    middle_ref[...] = middle
    n2 = (middle * rms(middle) * gains[3:4, :]).astype(BF)
    n2_ref[...] = n2
    out[...] = (middle + ffn_forward(n2, (w, v))).T


def ffn_grads(branch, n2, weights, dst):
    n2_grad = None
    for k in range(4):
        p = weights.at[k]
        gate = nt(n2, p[0:KW, :])
        up = nt(n2, p[KW : 2 * KW, :])
        s = jax.nn.sigmoid(gate)
        hidden = (gate * s * up).astype(BF)
        hidden_grad = nt(branch, p[2 * KW : 3 * KW, :])
        gate_grad = (hidden_grad * up * s * (1.0 + gate * (1.0 - s))).astype(BF)
        up_grad = (hidden_grad * gate * s).astype(BF)
        dst[k, 0:KW, :] = tn(gate_grad, n2).astype(BF)
        dst[k, KW : 2 * KW, :] = tn(up_grad, n2).astype(BF)
        dst[k, 2 * KW : 3 * KW, :] = tn(hidden, branch).astype(BF)
        term = nn(gate_grad, p[0:KW, :]) + nn(up_grad, p[KW : 2 * KW, :])
        n2_grad = term if n2_grad is None else n2_grad + term
    return n2_grad


def ffn_back_other_kernel(grad, n2, v, g_oth, part):
    part[...] = ffn_grads(grad[...].astype(BF), n2[...], v, g_oth)


def ffn_back_own_kernel(
    gain_row, grad, n2, w, half_grad, middle, att, wo, gains, g_own, mid_grad, d_out, d_wo, d_gain
):
    g = grad[...]
    n2_grad = half_grad[...] + ffn_grads(g.astype(BF), n2[...], w, g_own)
    part, gain_grad = norm_back(middle[...], gains[gain_row + 1 : gain_row + 2, :], n2_grad)
    m_grad = g + part
    mid_grad[...] = m_grad
    d_gain[...] = jnp.broadcast_to(gain_grad, (8, D))
    ab = m_grad.astype(BF)
    d_wo[...] = tn(att[...], ab).astype(BF)
    d_out[...] = nt(ab, wo[...]).astype(BF)


def attend_back_kernel(
    tab, own_pos, q, d_out, kp, vp, ot, lse, cos, sin, dkv_own, dkv_oth, dq_pre,
    qbd, dbd, dk, dv, dqt, flat,
):
    dk[...] = jnp.zeros(dk.shape, F32)
    dv[...] = jnp.zeros(dv.shape, F32)
    flat[:, D:] = jnp.zeros((ROWS, 64), F32)
    for block in range(2):
        position = own_pos[block]
        spread(q, qbd, block)
        spread(d_out, dbd, block)
        delta = jnp.sum(ot[block] * dbd[...].astype(F32).T, axis=0, keepdims=True)
        log_total = lse[block][0:1, :]
        dqt[...] = jnp.zeros((KW, D), F32)

        def step(i, masked):
            at = pl.ds(pl.multiple_of(i * CH_BACK, CH_BACK), CH_BACK)
            p = jnp.exp(nt(kp[at, :], qbd[...]) - log_total)
            if masked:
                p = jnp.where(allowed(i, position, CH_BACK), p, 0.0)
            p_grad = nt(vp[at, :], dbd[...])
            s_grad = (p * (p_grad - delta)).astype(BF)
            dv[at, :] += nn(p.astype(BF), dbd[...])
            dk[at, :] += nn(s_grad, qbd[...])
            dqt[...] += tn(kp[at, :], s_grad)

        def loop(i, carry):
            step(i, False)
            return carry

        last = position // (CH_BACK // BLK)
        lax.fori_loop(0, last, loop, 0)
        step(last, True)
        turned = (dqt[...] * (HD**-0.5)).T
        for h in range(HQ):
            g = h // 3
            flat[BLK * block : BLK * block + BLK, HD * h : HD * h + HD] = turned[
                HD * h : HD * h + HD, HD * g : HD * g + HD
            ]
    dq_pre[...] = spin(flat[...], cos[...], sin[...], True)[:, :D].astype(BF)

    def place(i, carry):
        for k in range(8):
            s = 8 * i + k
            to = pl.ds(pl.multiple_of(s * BLK, BLK), BLK)
            for base, ref in ((0, dkv_own), (32, dkv_oth)):
                at = pl.ds(pl.multiple_of(tab[base + s] * BLK, BLK), BLK)
                ref[to, :] = jnp.concatenate([dk[at, :].astype(BF), dv[at, :].astype(BF)], 1)
        return carry

    lax.fori_loop(0, 4, place, 0)


def project_back_kernel(
    gain_row, place_ref, t0, t1, t2, t3, dq_pre, normed, stream, gains, wqkv, mid_grad,
    d_wo, d_gain_two, cos, sin, grad, g_own, g_oth, kbuf, full, side,
):
    x, c = place_ref[0], place_ref[1]
    dkv = t0[...].astype(F32) + t1[...].astype(F32) + t2[...].astype(F32) + t3[...].astype(F32)
    kbuf[:, :KW] = dkv[:, :KW]
    kbuf[:, KW:] = jnp.zeros((ROWS, 64), F32)
    dk_pre = spin(kbuf[...], cos[...], sin[...], True)[:, :KW].astype(BF)
    dqk = jnp.concatenate([dq_pre[...], dk_pre], 1)
    dv_pre = dkv[:, KW:].astype(BF)
    n = normed[...]
    full[0] = tn(n, dq_pre[...]).astype(BF)
    full[1] = d_wo[...]
    side[:, : 2 * KW] = tn(n, jnp.concatenate([dk_pre, dv_pre], 1)).astype(BF)
    side[:, 2 * KW :] = jnp.zeros((D, KW), BF)
    n_grad = nt(jnp.concatenate([dqk, dv_pre], 1), wqkv[...])
    part, gain_grad = norm_back(stream[...].astype(F32), gains[gain_row : gain_row + 1, :], n_grad)
    total_grad = mid_grad[...] + part
    grad[...] = total_grad.T if grad.shape[0] == D else total_grad
    row = lax.broadcasted_iota(jnp.int32, (16, D), 0)
    both_gains = jnp.where(row == 0, gain_grad, d_gain_two[0:1, :]).astype(BF)

    def write(low, high):
        for j in range(4):
            start = pl.multiple_of(lax.rem(x + (OFFS[j] + 4), 4) * 144, 16)
            low[j, :144, :] = full[0, pl.ds(start, 144), :]
            high[j, :144, :] = full[1, pl.ds(start, 144), :]
            low[j, 144:, :] = side[pl.ds(start, 80), :]
            high[j, 144:208, :] = side[pl.ds(start + 80, 64), :]
            high[j, 208:, :] = both_gains

    @pl.when(c == 0)
    def _():
        write(g_own, g_oth)

    @pl.when(c == 1)
    def _():
        write(g_oth, g_own)


def pack_kernel(place, *refs):
    ffn0, ffn1, attn1, attn0, outs, tmp = *refs[:3], refs[3:7], refs[7:11], refs[11]
    tmp[:D, :] = ffn0[...]
    tmp[D : 2 * D, :] = ffn1[...]
    tmp[2 * D : 2 * D + 224, :] = sum(r[...].astype(F32) for r in attn0).astype(BF)
    tmp[2 * D + 224 :, :] = attn1[...]
    for j in range(4):
        start = lax.rem(place[2] + (OFFS[j] + 4), 4) * (PACK // 4)
        outs[j][...] = tmp[pl.ds(pl.multiple_of(start, 16), PACK // 4), :]


def unpack_kernel(
    place, m0, m1, m2, m3, t0, t1, t2, t3,
    dq, dk, dv, do, dg, du, dd, gains, mine, theirs, turn,
):
    c = place[1]
    for j in range(4):
        start = lax.rem(place[2] + (OFFS[j] + 4), 4) * (PACK // 4)
        mine[pl.ds(pl.multiple_of(start, 16), PACK // 4), :] = (m0, m1, m2, m3)[j][...]
        start = lax.rem(place[3] + (OFFS[j] + 4), 4) * (PACK // 4)
        theirs[pl.ds(pl.multiple_of(start, 16), PACK // 4), :] = (t0, t1, t2, t3)[j][...]
    for layer in range(2):
        a, b = mine.at[D * layer : D * layer + D], theirs.at[D * layer : D * layer + D]
        at_a = pl.ds(pl.multiple_of(c * KW, 64), KW)
        at_b = pl.ds(pl.multiple_of((1 - c) * KW, 64), KW)
        for k, ref in enumerate((dg, du, dd)):
            turn[at_a, :] = a[KW * k : KW * k + KW, :].astype(F32)
            turn[at_b, :] = b[KW * k : KW * k + KW, :].astype(F32)
            ref[layer] = turn[...].T

    def write(low, high):
        for layer in range(2):
            at = 2 * D + 224 * layer
            dq[layer] = low[at : at + 144, :].astype(F32)
            do[layer] = high[at : at + 144, :].astype(F32)
            for ref, lanes in ((dk, slice(0, KW)), (dv, slice(KW, 2 * KW))):
                ref[layer, :80, :] = low[at + 144 : at + 224, lanes].astype(F32)
                ref[layer, 80:, :] = high[at + 144 : at + 208, lanes].astype(F32)
            gains[8 * layer : 8 * layer + 8, :] = high[at + 208 : at + 224, :].astype(F32)[:8, :]

    @pl.when(c == 0)
    def _():
        write(mine, theirs)

    @pl.when(c == 1)
    def _():
        write(theirs, mine)


def local(tokens, pairing, cotangent, w_query, w_key, w_value, w_out, w_gate, w_up, w_down, attn_gain, ffn_gain):
    ctx = lax.axis_index("ctx")
    x = lax.axis_index("fsdp")
    z, y, c = ctx // 8, (ctx // 2) % 4, ctx % 2

    gains_in = jnp.stack([attn_gain[0], ffn_gain[0], attn_gain[1], ffn_gain[1]], 1)
    bundle = jnp.concatenate(
        [w_query[0], w_key[0], w_value[0], gains_in, jnp.zeros((144, 60), BF)], 1
    )
    first_pieces = gather_stage(bundle, along_x)
    outs = jnp.concatenate([w_out[0], w_out[1]], 1)
    later = jnp.concatenate([w_query[1], w_key[1], w_value[1], jnp.zeros((144, KW), BF)], 1)
    rest = gather_stage(jnp.where(c == 0, outs, later), along_x)

    def halves(layer):
        parts = [
            lax.dynamic_slice_in_dim(m, KW * c, KW, 0)
            for m in (w_gate[layer].T, w_up[layer].T, w_down[layer])
        ]
        return jnp.concatenate(parts, 0)

    def gather_ffn(mine):
        return lax.all_gather(mine, "fsdp", axis=0)

    spot = jnp.arange(16, dtype=jnp.int32)
    step = jnp.array(OFFS, jnp.int32)
    inner, outer = step[spot % 4], step[spot // 4]

    def owners(core):
        along_y = jnp.where(core == 0, inner, outer)
        along_z = jnp.where(core == 0, outer, inner)
        return ((z + along_z) % 4) * 8 + ((y + along_y) % 4) * 2 + core

    owner = jnp.concatenate([owners(c), owners(1 - c)])
    tab = pairing.reshape(32, 2)[owner].reshape(64)
    own_pos = lax.dynamic_slice_in_dim(pairing, 2 * ctx, 2)
    rows = (own_pos[:, None] * BLK + jnp.arange(BLK, dtype=jnp.int32)[None, :]).reshape(ROWS)
    frequency = BASE ** (-(jnp.arange(HD // 2, dtype=F32) * 2.0 / HD))
    angle = rows.astype(F32)[:, None] * frequency[None, :]
    cos1, sin1 = jnp.cos(angle), jnp.sin(angle)
    cos = jnp.concatenate([cos1] * 4, 1)
    sin = jnp.concatenate([-sin1, sin1] * 2, 1)
    spots = [x, c, jnp.where(c == 0, y, z), jnp.where(c == 0, z, y)]
    place = jnp.stack(spots).astype(jnp.int32)

    act = (ROWS, D)
    stream0 = tokens[0]
    normed0, q0, kv0, wqkv0, gains = call(
        first_kernel,
        [(act, BF), (act, BF), ((ROWS, 384), BF), ((D, 960), BF), ((8, D), F32)],
        [place, stream0, *first_pieces, cos, sin],
        smem=1,
        scratch=[pltpu.VMEM((D, 1024), BF)],
        us=3.0,
        name="project_first",
    )

    def attend(q, kv):
        return call(
            attend_kernel,
            [
                ((SEQ, KW), BF),
                ((SEQ, KW), BF),
                ((2, KW, D), F32),
                ((2, 8, D), F32),
                (act, BF),
            ],
            [tab, own_pos, q, *kv],
            smem=2,
            scratch=[pltpu.VMEM((D, KW), BF), pltpu.VMEM((KW, D), F32), pltpu.VMEM((8, D), F32)],
            us=12.0,
            name="attend",
        )

    ffn0 = gather_ffn(halves(0))
    kv0, first0 = gather_plane(kv0)
    ffn1 = gather_ffn(after(halves(1), first0))
    ffn0 = [ffn0, send(after(ffn0, *kv0), other_core)]
    kp0, vp0, ot0, lse0, att0 = attend(q0, kv0)
    rest = rest + swap([after(r, att0) for r in rest])
    middle0, n20, stream1, normed1, q1, kv1, wo0, wqkv1, wo1 = call(
        middle_first_kernel,
        [
            (act, F32),
            (act, BF),
            (act, F32),
            (act, BF),
            (act, BF),
            ((ROWS, 384), BF),
            ((D, D), BF),
            ((D, 960), BF),
            ((D, D), BF),
        ],
        [place, stream0, att0, gains, *ffn0, *rest, cos, sin],
        smem=1,
        us=8.0,
        name="middle_first",
    )
    kv1, _ = gather_plane(kv1)
    ffn1 = [ffn1, send(after(ffn1, *kv1), other_core)]
    kp1, vp1, ot1, lse1, att1 = attend(q1, kv1)
    middle1, n21, out = call(
        middle_last_kernel,
        [(act, F32), (act, BF), ((D, ROWS), F32)],
        [stream1, att1, wo1, gains, *ffn1],
        us=6.0,
        name="middle_last",
    )

    def ffn_back(layer, grad, middle, n2, att, wo, ffn, waits=()):
        g_oth, part = call(
            ffn_back_other_kernel,
            [((4, D, D), BF), (act, F32)],
            [grad, n2, ffn[1]],
            us=5.0,
            name="ffn_back_other",
        )
        g_oth = send(g_oth, other_core)
        g_own, mid_grad, d_out, *small = call(
            functools.partial(ffn_back_own_kernel, 2 * layer),
            [((4, D, D), BF), (act, F32), (act, BF), ((D, D), BF), ((8, D), F32)],
            [grad, n2, ffn[0], after(part, *waits), middle, att, wo, gains],
            us=6.0,
            name="ffn_back_own",
        )
        half = total([g_own, g_oth]).astype(BF)
        return after(d_out, half), half, mid_grad, small

    def attend_back(q, d_out, kp, vp, ot, lse):
        return call(
            attend_back_kernel,
            [((2048, 384), BF), ((2048, 384), BF), (act, BF)],
            [tab, own_pos, q, d_out, kp, vp, ot, lse, cos, sin],
            smem=2,
            scratch=[
                pltpu.VMEM((D, KW), BF),
                pltpu.VMEM((D, KW), BF),
                pltpu.VMEM((SEQ, KW), F32),
                pltpu.VMEM((SEQ, KW), F32),
                pltpu.VMEM((KW, D), F32),
                pltpu.VMEM((ROWS, 640), F32),
            ],
            us=20.0,
            name="attend_back",
        )

    def project_back(layer, terms, dq_pre, normed, stream, wqkv, mid_grad, d_wo, d_gain_two):
        return call(
            functools.partial(project_back_kernel, 2 * layer),
            [((D, ROWS) if layer == 0 else act, F32), ((4, 224, D), BF), ((4, 224, D), BF)],
            [place, *terms, dq_pre, normed, stream, gains, wqkv, mid_grad, d_wo, d_gain_two, cos, sin],
            smem=1,
            scratch=[
                pltpu.VMEM((ROWS, 256), F32),
                pltpu.VMEM((2, D, D), BF),
                pltpu.VMEM((D, D), BF),
            ],
            us=5.0,
            name="project_back",
        )

    def share(half, order):
        return scatter_stage([half[j] for j in order], along_x)

    owners_x = [(x + k) % 4 for k in OFFS]

    d_out, half, mid_grad, small = ffn_back(1, cotangent[0], middle1, n21, att1, wo1, ffn1)
    g_ffn1 = share(half, owners_x)
    dkv_own, dkv_oth, dq_pre = attend_back(q1, d_out, kp1, vp1, ot1, lse1)
    terms = scatter_plane(dkv_own, after(dkv_oth, *g_ffn1[1:3]))
    grad1, a_own, a_oth = project_back(
        1, terms, dq_pre, normed1, stream1, wqkv1, mid_grad, *small
    )

    half_attn = add_cores(a_own, a_oth)
    g_attn1 = share(half_attn, range(4))
    d_out, half, mid_grad, small = ffn_back(
        0, after(grad1, g_ffn1[3]), middle0, n20, att0, wo0, ffn0, [half_attn]
    )
    g_ffn0 = share(half, owners_x)
    dkv_own, dkv_oth, dq_pre = attend_back(q0, after(d_out, *g_attn1), kp0, vp0, ot0, lse0)
    terms = scatter_plane(dkv_own, after(dkv_oth, *g_ffn0[1:3]))
    grad0, a_own, a_oth = project_back(
        0, terms, dq_pre, normed0, stream0, wqkv0, mid_grad, *small
    )
    g_attn0 = share(add_cores(a_own, after(a_oth, g_ffn0[3])), range(4))

    cut = call(
        pack_kernel,
        [((PACK // 4, D), BF)] * 4,
        [place, *(total(g).astype(BF) for g in (g_ffn0, g_ffn1, g_attn1)), *g_attn0],
        smem=1,
        scratch=[pltpu.VMEM((PACK, D), BF)],
        us=3.0,
        name="pack",
    )
    piece = total(scatter_stage(cut, plane_one)).astype(BF)
    piece = total(gather_stage(piece, plane_two)).astype(BF)
    mine = gather_stage(piece, plane_one)
    *grads, gain_sums = call(
        unpack_kernel,
        [
            ((2, 144, D), F32),
            ((2, 144, KW), F32),
            ((2, 144, KW), F32),
            ((2, 144, D), F32),
            ((2, D, 384), F32),
            ((2, D, 384), F32),
            ((2, D, 384), F32),
            ((16, D), F32),
        ],
        [place, *mine, *swap(mine)],
        smem=1,
        scratch=[pltpu.VMEM((PACK, D), BF), pltpu.VMEM((PACK, D), BF), pltpu.VMEM((384, D), F32)],
        us=6.0,
        name="unpack",
    )
    own_gains = lax.dynamic_slice_in_dim(gain_sums, 144 * x, 144, 1).reshape(2, 8, 144)
    grads[6] = jnp.swapaxes(grads[6], 1, 2)
    return (out.T[None], grad0.T[None], *grads, own_gains[:, 0], own_gains[:, 1])


def solution(mesh):
    rows = P("fsdp", "ctx", None)
    wide = P(None, "fsdp", None)
    deep = P(None, None, "fsdp")
    flat = P(None, "fsdp")
    return jax.shard_map(
        local,
        mesh=mesh,
        in_specs=(rows, P(), rows, wide, wide, wide, wide, deep, deep, wide, flat, flat),
        out_specs=(rows, rows, wide, wide, wide, wide, deep, deep, wide, flat, flat),
        check_vma=False,
    )
```

```python
import functools

import jax
import jax.numpy as jnp
from jax import lax
from jax.experimental import pallas as pl
from jax.experimental.pallas import tpu as pltpu
from jax.sharding import PartitionSpec as P

D = 576
HQ = 9
HK = 3
HD = 64
FF = 1536
BLK = 64
ROWS = 128
SEQ = 4096
KW = 192
CH_FORWARD = 512
CH_BACK = 512
EPS = 1e-05
BASE = 100000.0
NEG = -1e30
F32 = jnp.float32
BF = jnp.bfloat16
AXES = ("ctx", "fsdp")
OFFS = (0, -1, 1, 2)
PACK = 2 * D + 2 * 224


def nn(a, b):
    return lax.dot_general(a, b, (((1,), (0,)), ((), ())), preferred_element_type=F32)


def nt(a, b):
    return lax.dot_general(a, b, (((1,), (1,)), ((), ())), preferred_element_type=F32)


def tn(a, b):
    return lax.dot_general(a, b, (((0,), (0,)), ((), ())), preferred_element_type=F32)


def pairs(move):
    found = []
    for z in range(4):
        for y in range(4):
            for c in range(2):
                for x in range(4):
                    a, b, e, f = move(z, y, c, x)
                    found.append(
                        (
                            ((z * 4 + y) * 2 + c) * 4 + x,
                            (((a % 4) * 4 + b % 4) * 2 + e) * 4 + f % 4,
                        )
                    )
    return found


def send(value, move):
    return lax.ppermute(value, AXES, pairs(move))


def plane(stage, k):
    def move(z, y, c, x):
        if (c + stage) % 2 == 0:
            return z, y + k, c, x
        return z + k, y, c, x

    return move


def along_x(k):
    return lambda z, y, c, x: (z, y, c, x + k)


def other_core(z, y, c, x):
    return z, y, 1 - c, x


def gather_stage(value, shift):
    return [value, send(value, shift(1)), send(value, shift(-1)), send(value, shift(2))]


def scatter_stage(parts, shift):
    return [
        parts[0],
        send(parts[1], shift(-1)),
        send(parts[2], shift(1)),
        send(parts[3], shift(2)),
    ]


def after(value, *others):
    return lax.optimization_barrier((value, *others))[0]


def total(parts):
    return sum(p.astype(F32) for p in parts)


def plane_one(k):
    return plane(0, k)


def plane_two(k):
    return plane(1, k)


def swap(values):
    return [send(v, other_core) for v in values]


def gather_plane(value):
    first = jnp.concatenate(gather_stage(value, plane_one), 0)
    own = gather_stage(first, plane_two)
    return own + swap(own), first


def scatter_plane(own, other):
    both = total([own, send(other, other_core)]).astype(BF)
    parts = both.reshape((4, 512) + own.shape[1:])
    one = total(scatter_stage([parts[j] for j in range(4)], plane_two)).astype(BF)
    one = one.reshape((4, 128) + own.shape[1:])
    return scatter_stage([one[j] for j in range(4)], plane_one)


def add_cores(own, other):
    return total([own, send(other, other_core)]).astype(BF)


def call(body, outs, args, smem=0, scratch=(), us=5.0, name=None):
    specs = [pl.BlockSpec(memory_space=pltpu.SMEM)] * smem
    specs += [pl.BlockSpec(memory_space=pltpu.VMEM)] * (len(args) - smem)
    return pl.pallas_call(
        body,
        out_shape=[jax.ShapeDtypeStruct(s, d) for s, d in outs],
        in_specs=specs,
        out_specs=[pl.BlockSpec(memory_space=pltpu.VMEM)] * len(outs),
        scratch_shapes=list(scratch),
        compiler_params=pltpu.CompilerParams(vmem_limit_bytes=58 * 1024 * 1024),
        cost_estimate=pl.CostEstimate(
            flops=int(us * 1.1e9), bytes_accessed=1000000, transcendentals=0
        ),
        name=name,
    )(*args)


def call_shares(body, outs, args, scratch=(), us=5.0, name=None):
    def spec(shape):
        if shape == (4, D, D):
            return pl.BlockSpec((1, D, D), lambda k: (k, 0, 0))
        return pl.BlockSpec(shape, lambda k: (0,) * len(shape))

    return pl.pallas_call(
        body,
        grid=(4,),
        out_shape=[jax.ShapeDtypeStruct(s, d) for s, d in outs],
        in_specs=[spec(a.shape) for a in args],
        out_specs=[spec(s) for s, _ in outs],
        scratch_shapes=list(scratch),
        compiler_params=pltpu.CompilerParams(vmem_limit_bytes=58 * 1024 * 1024),
        cost_estimate=pl.CostEstimate(
            flops=int(us * 1.1e9), bytes_accessed=1000000, transcendentals=0
        ),
        name=name,
    )(*args)


def spin(v, cos, sin, back=False):
    lane = lax.broadcasted_iota(jnp.int32, (v.shape[0], 128), 1)
    low = (lane % 64) < 32
    pieces = []
    for j in range(v.shape[1] // 128):
        part = v[:, 128 * j : 128 * j + 128]
        swapped = jnp.where(low, pltpu.roll(part, 96, 1), pltpu.roll(part, 32, 1))
        if back:
            pieces.append(part * cos - swapped * sin)
        else:
            pieces.append(part * cos + swapped * sin)
    return jnp.concatenate(pieces, 1)


def rms(x):
    return lax.rsqrt(jnp.mean(x * x, axis=-1, keepdims=True) + EPS)


def norm_back(x, gain, grad):
    r = rms(x)
    inner = jnp.mean(grad * gain * x, axis=-1, keepdims=True)
    d_x = r * gain * grad - x * (r * r * r * inner)
    d_gain = jnp.sum(grad * x * r, axis=0, keepdims=True)
    return d_x, d_gain


def project(normed, weight, cos, sin, q_ref, kv_ref):
    mixed = nn(normed, weight)
    turned = spin(mixed[:, :768], cos, sin)
    q_ref[...] = (turned[:, :D].astype(BF).astype(F32) * (HD**-0.5)).astype(BF)
    kv_ref[:, :KW] = turned[:, D:768].astype(BF)
    kv_ref[:, KW:] = mixed[:, 768:960].astype(BF)


def first_kernel(x_ref, tok, p0, p1, p2, p3, cos, sin, normed, q, kv, w, gains, tmp):
    for j, piece in enumerate((p0, p1, p2, p3)):
        owner = lax.rem(x_ref[0] + (OFFS[j] + 4), 4)
        tmp[pl.ds(pl.multiple_of(owner * 144, 16), 144), :] = piece[...]
    w[...] = tmp[:, :960]
    g = tmp[:, 896:1024].astype(F32).T
    gains[...] = g[64:72, :]
    x = tok[...].astype(F32)
    n = (x * rms(x) * g[64:65, :]).astype(BF)
    normed[...] = n
    project(n, w[...], cos[...], sin[...], q, kv)


def spread(src, dst, block):
    dst[...] = jnp.zeros(dst.shape, BF)
    for h in range(HQ):
        g = h // 3
        dst[HD * h : HD * h + HD, HD * g : HD * g + HD] = src[
            BLK * block : BLK * block + BLK, HD * h : HD * h + HD
        ]


def allowed(chunk, position, size):
    key = lax.broadcasted_iota(jnp.int32, (size, D), 0) + chunk * size
    query = (lax.broadcasted_iota(jnp.int32, (size, D), 1) % BLK) + position * BLK
    return key <= query


def attend_kernel(tab, own_pos, q, *rest):
    kv, (kp, vp, ot, lse, att, qbd, acc, stat) = rest[:8], rest[8:]

    def place(s, carry):
        for j, ref in enumerate(kv):
            at = pl.ds(pl.multiple_of(tab[8 * j + s] * BLK, BLK), BLK)
            rows = ref[pl.ds(pl.multiple_of(s * BLK, BLK), BLK), :]
            kp[at, :] = rows[:, :KW]
            vp[at, :] = rows[:, KW:]
        return carry

    lax.fori_loop(0, 8, place, 0)
    for block in range(2):
        position = own_pos[block]
        spread(q, qbd, block)
        stat[0:1, :] = jnp.full((1, D), NEG, F32)
        stat[1:2, :] = jnp.zeros((1, D), F32)
        acc[...] = jnp.zeros((KW, D), F32)

        def step(i, masked):
            at = pl.ds(pl.multiple_of(i * CH_FORWARD, CH_FORWARD), CH_FORWARD)
            s = nt(kp[at, :], qbd[...])
            if masked:
                s = jnp.where(allowed(i, position, CH_FORWARD), s, NEG)
            old = stat[0:1, :]
            new = jnp.maximum(old, jnp.max(s, axis=0, keepdims=True))
            p = jnp.exp(s - new)
            fade = jnp.exp(old - new)
            stat[0:1, :] = new
            stat[1:2, :] = stat[1:2, :] * fade + jnp.sum(p, axis=0, keepdims=True)
            acc[...] = acc[...] * fade + tn(vp[at, :], p.astype(BF))

        def loop(i, carry):
            step(i, False)
            return carry

        last = position // (CH_FORWARD // BLK)
        lax.fori_loop(0, last, loop, 0)
        step(last, True)
        result = acc[...] / stat[1:2, :]
        ot[block] = result
        lse[block] = jnp.broadcast_to(stat[0:1, :] + jnp.log(stat[1:2, :]), (8, D))
        turned = result.T
        for h in range(HQ):
            g = h // 3
            att[BLK * block : BLK * block + BLK, HD * h : HD * h + HD] = turned[
                HD * h : HD * h + HD, HD * g : HD * g + HD
            ].astype(BF)


def ffn_forward(n2, pieces):
    out = None
    for ref in pieces:
        for k in range(4):
            gate = nt(n2, ref[k, 0:KW, :])
            up = nt(n2, ref[k, KW : 2 * KW, :])
            hidden = (gate * jax.nn.sigmoid(gate) * up).astype(BF)
            term = nn(hidden, ref[k, 2 * KW : 3 * KW, :])
            out = term if out is None else out + term
    return out


def middle_first_kernel(
    place, stream, att, gains, w, v, r0, r1, r2, r3, s0, s1, s2, s3, cos, sin,
    middle_ref, n2_ref, out, normed, q, kv, wo0, wqkv1, wo1,
):
    x, c = place[0], place[1]

    def sort(outs, projections):
        for j in range(4):
            owner = lax.rem(x + (OFFS[j] + 4), 4)
            at = pl.ds(pl.multiple_of(owner * 144, 16), 144)
            wo0[at, :] = outs[j][:, :D]
            wo1[at, :] = outs[j][:, D:]
            wqkv1[at, :] = projections[j][:, :960]

    @pl.when(c == 0)
    def _():
        sort((r0, r1, r2, r3), (s0, s1, s2, s3))

    @pl.when(c == 1)
    def _():
        sort((s0, s1, s2, s3), (r0, r1, r2, r3))

    middle = stream[...].astype(F32) + nn(att[...], wo0[...])
    middle_ref[...] = middle
    n2 = (middle * rms(middle) * gains[1:2, :]).astype(BF)
    n2_ref[...] = n2
    result = middle + ffn_forward(n2, (w, v))
    out[...] = result
    n = (result * rms(result) * gains[2:3, :]).astype(BF)
    normed[...] = n
    project(n, wqkv1[...], cos[...], sin[...], q, kv)


def middle_last_kernel(stream, att, wo, gains, w, v, middle_ref, n2_ref, out):
    middle = stream[...] + nn(att[...], wo[...])
    middle_ref[...] = middle
    n2 = (middle * rms(middle) * gains[3:4, :]).astype(BF)
    n2_ref[...] = n2
    out[...] = (middle + ffn_forward(n2, (w, v))).T


def ffn_grads(branch, n2, p, dst):
    gate = nt(n2, p[0, 0:KW, :])
    up = nt(n2, p[0, KW : 2 * KW, :])
    s = jax.nn.sigmoid(gate)
    hidden = (gate * s * up).astype(BF)
    hidden_grad = nt(branch, p[0, 2 * KW : 3 * KW, :])
    gate_grad = (hidden_grad * up * s * (1.0 + gate * (1.0 - s))).astype(BF)
    up_grad = (hidden_grad * gate * s).astype(BF)
    dst[0, 0:KW, :] = tn(gate_grad, n2).astype(BF)
    dst[0, KW : 2 * KW, :] = tn(up_grad, n2).astype(BF)
    dst[0, 2 * KW : 3 * KW, :] = tn(hidden, branch).astype(BF)
    return nn(gate_grad, p[0, 0:KW, :]) + nn(up_grad, p[0, KW : 2 * KW, :])


def ffn_back_other_kernel(grad, n2, v, g_oth, part):
    @pl.when(pl.program_id(0) == 0)
    def _():
        part[...] = jnp.zeros((ROWS, D), F32)

    part[...] += ffn_grads(grad[...].astype(BF), n2[...], v, g_oth)


def ffn_back_own_kernel(
    gain_row, grad, n2, w, half_grad, middle, att, wo, gains,
    g_own, mid_grad, d_out, d_wo, d_gain, acc,
):
    g = grad[...]

    @pl.when(pl.program_id(0) == 0)
    def _():
        acc[...] = half_grad[...]

    acc[...] += ffn_grads(g.astype(BF), n2[...], w, g_own)

    @pl.when(pl.program_id(0) == 3)
    def _():
        gain = gains[gain_row + 1 : gain_row + 2, :]
        part, gain_grad = norm_back(middle[...], gain, acc[...])
        m_grad = g + part
        mid_grad[...] = m_grad
        d_gain[...] = jnp.broadcast_to(gain_grad, (8, D))
        ab = m_grad.astype(BF)
        d_wo[...] = tn(att[...], ab).astype(BF)
        d_out[...] = nt(ab, wo[...]).astype(BF)


def attend_back_kernel(
    tab, own_pos, q, d_out, kp, vp, ot, lse, cos, sin, dkv_own, dkv_oth, dq_pre,
    qbd, dbd, dk, dv, dqt, flat,
):
    dk[...] = jnp.zeros(dk.shape, F32)
    dv[...] = jnp.zeros(dv.shape, F32)
    flat[:, D:] = jnp.zeros((ROWS, 64), F32)
    for block in range(2):
        position = own_pos[block]
        spread(q, qbd, block)
        spread(d_out, dbd, block)
        delta = jnp.sum(ot[block] * dbd[...].astype(F32).T, axis=0, keepdims=True)
        log_total = lse[block][0:1, :]
        dqt[...] = jnp.zeros((KW, D), F32)

        def step(i, masked):
            at = pl.ds(pl.multiple_of(i * CH_BACK, CH_BACK), CH_BACK)
            p = jnp.exp(nt(kp[at, :], qbd[...]) - log_total)
            if masked:
                p = jnp.where(allowed(i, position, CH_BACK), p, 0.0)
            p_grad = nt(vp[at, :], dbd[...])
            s_grad = (p * (p_grad - delta)).astype(BF)
            dv[at, :] += nn(p.astype(BF), dbd[...])
            dk[at, :] += nn(s_grad, qbd[...])
            dqt[...] += tn(kp[at, :], s_grad)

        def loop(i, carry):
            step(i, False)
            return carry

        last = position // (CH_BACK // BLK)
        lax.fori_loop(0, last, loop, 0)
        step(last, True)
        turned = (dqt[...] * (HD**-0.5)).T
        for h in range(HQ):
            g = h // 3
            flat[BLK * block : BLK * block + BLK, HD * h : HD * h + HD] = turned[
                HD * h : HD * h + HD, HD * g : HD * g + HD
            ]
    dq_pre[...] = spin(flat[...], cos[...], sin[...], True)[:, :D].astype(BF)

    def place(i, carry):
        for k in range(8):
            s = 8 * i + k
            to = pl.ds(pl.multiple_of(s * BLK, BLK), BLK)
            for base, ref in ((0, dkv_own), (32, dkv_oth)):
                at = pl.ds(pl.multiple_of(tab[base + s] * BLK, BLK), BLK)
                ref[to, :] = jnp.concatenate([dk[at, :].astype(BF), dv[at, :].astype(BF)], 1)
        return carry

    lax.fori_loop(0, 4, place, 0)


def project_back_kernel(
    gain_row, place_ref, t0, t1, t2, t3, dq_pre, normed, stream, gains, wqkv, mid_grad,
    d_wo, d_gain_two, cos, sin, grad, g_own, g_oth, kbuf, full, side,
):
    x, c = place_ref[0], place_ref[1]
    dkv = t0[...].astype(F32) + t1[...].astype(F32) + t2[...].astype(F32) + t3[...].astype(F32)
    kbuf[:, :KW] = dkv[:, :KW]
    kbuf[:, KW:] = jnp.zeros((ROWS, 64), F32)
    dk_pre = spin(kbuf[...], cos[...], sin[...], True)[:, :KW].astype(BF)
    dqk = jnp.concatenate([dq_pre[...], dk_pre], 1)
    dv_pre = dkv[:, KW:].astype(BF)
    n = normed[...]
    full[0] = tn(n, dq_pre[...]).astype(BF)
    full[1] = d_wo[...]
    side[:, : 2 * KW] = tn(n, jnp.concatenate([dk_pre, dv_pre], 1)).astype(BF)
    side[:, 2 * KW :] = jnp.zeros((D, KW), BF)
    n_grad = nt(jnp.concatenate([dqk, dv_pre], 1), wqkv[...])
    part, gain_grad = norm_back(stream[...].astype(F32), gains[gain_row : gain_row + 1, :], n_grad)
    total_grad = mid_grad[...] + part
    grad[...] = total_grad.T if grad.shape[0] == D else total_grad
    row = lax.broadcasted_iota(jnp.int32, (16, D), 0)
    both_gains = jnp.where(row == 0, gain_grad, d_gain_two[0:1, :]).astype(BF)

    def write(low, high):
        for j in range(4):
            start = pl.multiple_of(lax.rem(x + (OFFS[j] + 4), 4) * 144, 16)
            low[j, :144, :] = full[0, pl.ds(start, 144), :]
            high[j, :144, :] = full[1, pl.ds(start, 144), :]
            low[j, 144:, :] = side[pl.ds(start, 80), :]
            high[j, 144:208, :] = side[pl.ds(start + 80, 64), :]
            high[j, 208:, :] = both_gains

    @pl.when(c == 0)
    def _():
        write(g_own, g_oth)

    @pl.when(c == 1)
    def _():
        write(g_oth, g_own)


def pack_kernel(place, *refs):
    ffn0, ffn1, attn1, attn0, outs, tmp = *refs[:3], refs[3:7], refs[7:11], refs[11]
    tmp[:D, :] = ffn0[...]
    tmp[D : 2 * D, :] = ffn1[...]
    tmp[2 * D : 2 * D + 224, :] = sum(r[...].astype(F32) for r in attn0).astype(BF)
    tmp[2 * D + 224 :, :] = attn1[...]
    for j in range(4):
        start = lax.rem(place[2] + (OFFS[j] + 4), 4) * (PACK // 4)
        outs[j][...] = tmp[pl.ds(pl.multiple_of(start, 16), PACK // 4), :]


def unpack_kernel(
    place, m0, m1, m2, m3, t0, t1, t2, t3,
    dq, dk, dv, do, dg, du, dd, gains, mine, theirs, turn,
):
    c = place[1]
    for j in range(4):
        start = lax.rem(place[2] + (OFFS[j] + 4), 4) * (PACK // 4)
        mine[pl.ds(pl.multiple_of(start, 16), PACK // 4), :] = (m0, m1, m2, m3)[j][...]
        start = lax.rem(place[3] + (OFFS[j] + 4), 4) * (PACK // 4)
        theirs[pl.ds(pl.multiple_of(start, 16), PACK // 4), :] = (t0, t1, t2, t3)[j][...]
    for layer in range(2):
        a, b = mine.at[D * layer : D * layer + D], theirs.at[D * layer : D * layer + D]
        at_a = pl.ds(pl.multiple_of(c * KW, 64), KW)
        at_b = pl.ds(pl.multiple_of((1 - c) * KW, 64), KW)
        for k, ref in enumerate((dg, du, dd)):
            turn[at_a, :] = a[KW * k : KW * k + KW, :].astype(F32)
            turn[at_b, :] = b[KW * k : KW * k + KW, :].astype(F32)
            ref[layer] = turn[...].T

    def write(low, high):
        for layer in range(2):
            at = 2 * D + 224 * layer
            dq[layer] = low[at : at + 144, :].astype(F32)
            do[layer] = high[at : at + 144, :].astype(F32)
            for ref, lanes in ((dk, slice(0, KW)), (dv, slice(KW, 2 * KW))):
                ref[layer, :80, :] = low[at + 144 : at + 224, lanes].astype(F32)
                ref[layer, 80:, :] = high[at + 144 : at + 208, lanes].astype(F32)
            gains[8 * layer : 8 * layer + 8, :] = high[at + 208 : at + 224, :].astype(F32)[:8, :]

    @pl.when(c == 0)
    def _():
        write(mine, theirs)

    @pl.when(c == 1)
    def _():
        write(theirs, mine)


def local(tokens, pairing, cotangent, w_query, w_key, w_value, w_out, w_gate, w_up, w_down, attn_gain, ffn_gain):
    ctx = lax.axis_index("ctx")
    x = lax.axis_index("fsdp")
    z, y, c = ctx // 8, (ctx // 2) % 4, ctx % 2

    gains_in = jnp.stack([attn_gain[0], ffn_gain[0], attn_gain[1], ffn_gain[1]], 1)
    bundle = jnp.concatenate(
        [w_query[0], w_key[0], w_value[0], gains_in, jnp.zeros((144, 60), BF)], 1
    )
    first_pieces = gather_stage(bundle, along_x)
    outs = jnp.concatenate([w_out[0], w_out[1]], 1)
    later = jnp.concatenate([w_query[1], w_key[1], w_value[1], jnp.zeros((144, KW), BF)], 1)
    rest = gather_stage(jnp.where(c == 0, outs, later), along_x)

    def halves(layer):
        parts = [
            lax.dynamic_slice_in_dim(m, KW * c, KW, 0)
            for m in (w_gate[layer].T, w_up[layer].T, w_down[layer])
        ]
        return jnp.concatenate(parts, 0)

    def gather_ffn(mine):
        return lax.all_gather(mine, "fsdp", axis=0)

    spot = jnp.arange(16, dtype=jnp.int32)
    step = jnp.array(OFFS, jnp.int32)
    inner, outer = step[spot % 4], step[spot // 4]

    def owners(core):
        along_y = jnp.where(core == 0, inner, outer)
        along_z = jnp.where(core == 0, outer, inner)
        return ((z + along_z) % 4) * 8 + ((y + along_y) % 4) * 2 + core

    owner = jnp.concatenate([owners(c), owners(1 - c)])
    tab = pairing.reshape(32, 2)[owner].reshape(64)
    own_pos = lax.dynamic_slice_in_dim(pairing, 2 * ctx, 2)
    rows = (own_pos[:, None] * BLK + jnp.arange(BLK, dtype=jnp.int32)[None, :]).reshape(ROWS)
    frequency = BASE ** (-(jnp.arange(HD // 2, dtype=F32) * 2.0 / HD))
    angle = rows.astype(F32)[:, None] * frequency[None, :]
    cos1, sin1 = jnp.cos(angle), jnp.sin(angle)
    cos = jnp.concatenate([cos1] * 4, 1)
    sin = jnp.concatenate([-sin1, sin1] * 2, 1)
    spots = [x, c, jnp.where(c == 0, y, z), jnp.where(c == 0, z, y)]
    place = jnp.stack(spots).astype(jnp.int32)

    act = (ROWS, D)
    stream0 = tokens[0]
    normed0, q0, kv0, wqkv0, gains = call(
        first_kernel,
        [(act, BF), (act, BF), ((ROWS, 384), BF), ((D, 960), BF), ((8, D), F32)],
        [place, stream0, *first_pieces, cos, sin],
        smem=1,
        scratch=[pltpu.VMEM((D, 1024), BF)],
        us=3.0,
        name="project_first",
    )

    def attend(q, kv):
        return call(
            attend_kernel,
            [
                ((SEQ, KW), BF),
                ((SEQ, KW), BF),
                ((2, KW, D), F32),
                ((2, 8, D), F32),
                (act, BF),
            ],
            [tab, own_pos, q, *kv],
            smem=2,
            scratch=[pltpu.VMEM((D, KW), BF), pltpu.VMEM((KW, D), F32), pltpu.VMEM((8, D), F32)],
            us=12.0,
            name="attend",
        )

    ffn0 = gather_ffn(halves(0))
    kv0, first0 = gather_plane(kv0)
    ffn1 = gather_ffn(after(halves(1), first0))
    ffn0 = [ffn0, send(after(ffn0, *kv0), other_core)]
    kp0, vp0, ot0, lse0, att0 = attend(q0, kv0)
    rest = rest + swap([after(r, att0) for r in rest])
    middle0, n20, stream1, normed1, q1, kv1, wo0, wqkv1, wo1 = call(
        middle_first_kernel,
        [
            (act, F32),
            (act, BF),
            (act, F32),
            (act, BF),
            (act, BF),
            ((ROWS, 384), BF),
            ((D, D), BF),
            ((D, 960), BF),
            ((D, D), BF),
        ],
        [place, stream0, att0, gains, *ffn0, *rest, cos, sin],
        smem=1,
        us=8.0,
        name="middle_first",
    )
    kv1, _ = gather_plane(kv1)
    ffn1 = [ffn1, send(after(ffn1, *kv1), other_core)]
    kp1, vp1, ot1, lse1, att1 = attend(q1, kv1)
    middle1, n21, out = call(
        middle_last_kernel,
        [(act, F32), (act, BF), ((D, ROWS), F32)],
        [stream1, att1, wo1, gains, *ffn1],
        us=6.0,
        name="middle_last",
    )

    def ffn_back(layer, grad, middle, n2, att, wo, ffn, waits=()):
        g_oth, part = call_shares(
            ffn_back_other_kernel,
            [((4, D, D), BF), (act, F32)],
            [grad, n2, ffn[1]],
            us=5.0,
            name="ffn_back_other",
        )
        g_oth = send(g_oth, other_core)
        g_own, mid_grad, d_out, *small = call_shares(
            functools.partial(ffn_back_own_kernel, 2 * layer),
            [((4, D, D), BF), (act, F32), (act, BF), ((D, D), BF), ((8, D), F32)],
            [grad, n2, ffn[0], after(part, *waits), middle, att, wo, gains],
            scratch=[pltpu.VMEM((ROWS, D), F32)],
            us=6.0,
            name="ffn_back_own",
        )
        half = total([g_own, g_oth]).astype(BF)
        return after(d_out, half), half, mid_grad, small

    def attend_back(q, d_out, kp, vp, ot, lse):
        return call(
            attend_back_kernel,
            [((2048, 384), BF), ((2048, 384), BF), (act, BF)],
            [tab, own_pos, q, d_out, kp, vp, ot, lse, cos, sin],
            smem=2,
            scratch=[
                pltpu.VMEM((D, KW), BF),
                pltpu.VMEM((D, KW), BF),
                pltpu.VMEM((SEQ, KW), F32),
                pltpu.VMEM((SEQ, KW), F32),
                pltpu.VMEM((KW, D), F32),
                pltpu.VMEM((ROWS, 640), F32),
            ],
            us=20.0,
            name="attend_back",
        )

    def project_back(layer, terms, dq_pre, normed, stream, wqkv, mid_grad, d_wo, d_gain_two):
        return call(
            functools.partial(project_back_kernel, 2 * layer),
            [((D, ROWS) if layer == 0 else act, F32), ((4, 224, D), BF), ((4, 224, D), BF)],
            [place, *terms, dq_pre, normed, stream, gains, wqkv, mid_grad, d_wo, d_gain_two, cos, sin],
            smem=1,
            scratch=[
                pltpu.VMEM((ROWS, 256), F32),
                pltpu.VMEM((2, D, D), BF),
                pltpu.VMEM((D, D), BF),
            ],
            us=5.0,
            name="project_back",
        )

    def share(half, order):
        return scatter_stage([half[j] for j in order], along_x)

    owners_x = [(x + k) % 4 for k in OFFS]

    d_out, half, mid_grad, small = ffn_back(1, cotangent[0], middle1, n21, att1, wo1, ffn1)
    g_ffn1 = share(half, owners_x)
    dkv_own, dkv_oth, dq_pre = attend_back(q1, d_out, kp1, vp1, ot1, lse1)
    terms = scatter_plane(dkv_own, after(dkv_oth, *g_ffn1[1:3]))
    grad1, a_own, a_oth = project_back(
        1, terms, dq_pre, normed1, stream1, wqkv1, mid_grad, *small
    )

    half_attn = add_cores(a_own, a_oth)
    g_attn1 = share(half_attn, range(4))
    d_out, half, mid_grad, small = ffn_back(
        0, after(grad1, g_ffn1[3]), middle0, n20, att0, wo0, ffn0, [half_attn]
    )
    g_ffn0 = share(half, owners_x)
    dkv_own, dkv_oth, dq_pre = attend_back(q0, after(d_out, *g_attn1), kp0, vp0, ot0, lse0)
    terms = scatter_plane(dkv_own, after(dkv_oth, *g_ffn0[1:3]))
    grad0, a_own, a_oth = project_back(
        0, terms, dq_pre, normed0, stream0, wqkv0, mid_grad, *small
    )
    g_attn0 = share(add_cores(a_own, after(a_oth, g_ffn0[3])), range(4))

    cut = call(
        pack_kernel,
        [((PACK // 4, D), BF)] * 4,
        [place, *(total(g).astype(BF) for g in (g_ffn0, g_ffn1, g_attn1)), *g_attn0],
        smem=1,
        scratch=[pltpu.VMEM((PACK, D), BF)],
        us=3.0,
        name="pack",
    )
    piece = total(scatter_stage(cut, plane_one)).astype(BF)
    piece = total(gather_stage(piece, plane_two)).astype(BF)
    mine = gather_stage(piece, plane_one)
    *grads, gain_sums = call(
        unpack_kernel,
        [
            ((2, 144, D), F32),
            ((2, 144, KW), F32),
            ((2, 144, KW), F32),
            ((2, 144, D), F32),
            ((2, D, 384), F32),
            ((2, D, 384), F32),
            ((2, D, 384), F32),
            ((16, D), F32),
        ],
        [place, *mine, *swap(mine)],
        smem=1,
        scratch=[pltpu.VMEM((PACK, D), BF), pltpu.VMEM((PACK, D), BF), pltpu.VMEM((384, D), F32)],
        us=6.0,
        name="unpack",
    )
    own_gains = lax.dynamic_slice_in_dim(gain_sums, 144 * x, 144, 1).reshape(2, 8, 144)
    grads[6] = jnp.swapaxes(grads[6], 1, 2)
    return (out.T[None], grad0.T[None], *grads, own_gains[:, 0], own_gains[:, 1])


def solution(mesh):
    rows = P("fsdp", "ctx", None)
    wide = P(None, "fsdp", None)
    deep = P(None, None, "fsdp")
    flat = P(None, "fsdp")
    return jax.shard_map(
        local,
        mesh=mesh,
        in_specs=(rows, P(), rows, wide, wide, wide, wide, deep, deep, wide, flat, flat),
        out_specs=(rows, rows, wide, wide, wide, wide, deep, deep, wide, flat, flat),
        check_vma=False,
    )
```
